256 devices in a mesh: dp: 64 (over x, z, core), section: 4 (over y).
Axes of the slice: x: 4, y: 4, z: 8, core: 2. Of those that a mesh axis runs over, the one named last changes fastest.
Arguments:
- acts: bfloat16 [4, 49152, 4608], P('section', 'dp'), may hold values from -16 to 16
- grad_out: bfloat16 [4, 49152, 512], P('section', 'dp'), may hold values from -0.02734375 to 0.02734375
- params: float32 [4, 18432, 128], P('section', 'dp'), may hold values from -0.3125 to 0.3125
- moment1: float32 [4, 18432, 128], P('section', 'dp'), may hold values from -4 to 4
- moment2: float32 [4, 18432, 128], P('section', 'dp'), may hold values from 0.01 to 0.1
- ema: float32 [4, 18432, 128], P('section', 'dp'), may hold values from -0.3125 to 0.3125
- live_rows: int32 [4], replicated, may hold values from 9216 to 18432
- home: int32 [4, 9], replicated, may hold values from 0 to 3, as said below
Outputs:
- new_params: float32 [4, 18432, 128], P('section', 'dp')
- new_moment1: float32 [4, 18432, 128], P('section', 'dp')
- new_moment2: float32 [4, 18432, 128], P('section', 'dp')
- new_ema: float32 [4, 18432, 128], P('section', 'dp')
- weights: bfloat16 [4, 4608, 512], P('section')
The draws below stay inside these ranges and needn't reach their ends.
Inputs may be any that keep to these rules, and one draw needn't show every extreme that they name: Every section is home of exactly 9 blocks.
All inputs are finite; a program needn't handle non-finite values.
Results may differ from the reference program's by a relative error of at most 0.0075.
Values may be sent and summed in bfloat16 or wider, within the bound.
A program may use at most 128 MiB of HBM per device.

```python
import math
import jax
import jax.numpy as jnp
from jax import lax

K = 4608
C = 512
N_GEN = 2
STEP = 100
BROWS = 32
TOKENS = 49152
ROWS = 18432
SHARD = 288
NBLK = 9
N_DP = 64
N_SECTION = 4


def draw_home(key, part):
    key = jax.random.fold_in(key, 7)
    shuffled = jax.random.permutation(key, N_SECTION * NBLK)
    return (shuffled // NBLK).reshape(N_SECTION, NBLK).astype(jnp.int32)


def plant(result, stream_key, smallest, high):
    spot = [jax.random.randint(jax.random.fold_in(stream_key, axis), (), 0, length) for axis, length in enumerate(result.shape)]
    main_axis = result.shape.index(max(result.shape))
    neighbour = spot[:main_axis] + [(spot[main_axis] + 1) % result.shape[main_axis]] + spot[main_axis + 1:]
    return result.at[tuple(spot)].set(smallest).at[tuple(neighbour)].set(high)


def with_spikes(array, key, source, target, shards_of, factor):
    owner, partner = [(jnp.arange(array.shape[dim]) // (array.shape[dim] // shards_of)).reshape([-1 if axis == dim else 1 for axis in range(array.ndim)]) for dim in (source, target)]
    chosen = jax.random.permutation(key, shards_of)[partner]
    strong = (owner == chosen) | (owner == (partner + shards_of // 2) % shards_of)
    return jnp.where(strong, factor * array, array)


def block_levels(stream_key, shape, pieces, least, high):
    level = 1.0
    for axis_at, parts in pieces:
        steps = jax.random.uniform(jax.random.fold_in(jax.random.fold_in(stream_key, 6), axis_at), (parts,), jnp.float32, least / len(pieces), high / len(pieces))
        level = level * jnp.repeat(jnp.exp(steps), shape[axis_at] // parts).reshape((-1,) + (1,) * (len(shape) - 1 - axis_at))
    return level


def normal_values(stream_key, dims, deviation, most, split=(), held_as=jnp.bfloat16):
    entries = jax.random.normal(stream_key, dims, jnp.float32) * deviation
    if len(split) > 0:
        entries = block_levels(stream_key, dims, split, -0.22, 0.18) * entries
    return jnp.clip(entries, min=-most, max=most).astype(held_as)


def heavy_noise(rng, dims, scale, limit, cuts, heavy, kind=jnp.bfloat16):
    result = scale * jax.random.normal(rng, dims, jnp.float32)
    if cuts:
        result = result * block_levels(rng, dims, cuts, -0.22, 0.18)
    return jnp.clip(with_spikes(result, jax.random.fold_in(rng, 3), *heavy), -limit, limit).astype(kind)


def setup_inputs(seed: int = 0) -> dict:
    splits = jax.random.split(jax.random.key(seed), 9)
    return {
        "acts": heavy_noise(splits[0], (N_SECTION, TOKENS, K), 1.0, 16.0, ((0, 4), (1, 64)), (1, 2, 64, 4.0)),
        "grad_out": normal_values(splits[1], (N_SECTION, TOKENS, C), TOKENS ** -0.5, 0.02734375, ((0, 4), (1, 64))),
        "params": normal_values(splits[2], (N_SECTION, ROWS, 128), 0.02, 0.3125, ((0, 4), (1, 64)), jnp.float32),
        "moment1": normal_values(splits[3], (N_SECTION, ROWS, 128), 1.0, 4.0, ((0, 4), (1, 64)), jnp.float32),
        "moment2": jnp.clip(jnp.exp(math.log(0.1) - 2.3025851 * jax.random.uniform(splits[4], (N_SECTION, ROWS, 128), jnp.float32) ** block_levels(splits[4], (N_SECTION, ROWS, 128), ((0, 4), (1, 64)), -0.2, 0.2)), 0.01, 0.1),
        "ema": normal_values(splits[5], (N_SECTION, ROWS, 128), 0.02, 0.3125, ((0, 4), (1, 64)), jnp.float32),
        "live_rows": plant(jax.random.randint(splits[6], (N_SECTION,), ROWS // 2, ROWS + 1), jax.random.fold_in(splits[6], 1), ROWS // 2, ROWS).astype(jnp.int32),
        "home": draw_home(jax.random.fold_in(splits[8], 71), 0),
    }


def home_tables(home, nblk):
    flat = home.reshape(-1).astype(jnp.int32)
    total = flat.shape[0]
    counter = jnp.arange(total, dtype=jnp.int32)
    earlier = (flat[None, :] == flat[:, None]) & (counter[None, :] < counter[:, None])
    ranks = lax.optimization_barrier(jnp.sum(earlier.astype(jnp.int32), axis=1)).astype(jnp.int32)
    position = (flat * nblk + ranks).astype(jnp.int32)
    order = lax.optimization_barrier(jnp.sum(jnp.where(position[None, :] == counter[:, None], counter[None, :], 0), axis=1)).astype(jnp.int32)
    return (position, order)

def adam_update(params, moment1, moment2, ema, grads, alive, generator):
    corr_one = 1.0 - 0.9 ** STEP
    corr_two = 1.0 - 0.99 ** STEP
    first = jnp.where(alive, 0.9 * moment1 + 0.1 * grads, moment1)
    second = jnp.where(alive, 0.99 * moment2 + 0.01 * grads * grads, moment2)
    stepped = params - 0.0025 * (first / corr_one) / (jnp.sqrt(second / corr_two) + 1e-08)
    updated = jnp.where(alive, stepped, params)
    averaged = jnp.where(generator, 0.995 * ema + 0.005 * updated, ema)
    return (updated, first, second, averaged)

def reference(acts, grad_out, params, moment1, moment2, ema, live_rows, home):
    position, order = home_tables(home, NBLK)
    stacked = []
    for section_id in range(N_SECTION):
        product = jnp.dot(acts[section_id].T, grad_out[section_id], preferred_element_type=jnp.float32)
        stacked.append(product.reshape(ROWS, 128))
    grads = jnp.stack(stacked).reshape(N_SECTION, N_DP, NBLK, BROWS, 128)
    grads = jnp.transpose(grads, (1, 0, 2, 3, 4)).reshape(N_DP, N_SECTION * NBLK, BROWS, 128)
    homed = grads[:, order]
    homed = jnp.transpose(homed.reshape(N_DP, N_SECTION, NBLK, BROWS, 128), (1, 0, 2, 3, 4)).reshape(N_SECTION, ROWS, 128)
    source = order // NBLK
    within = order % NBLK
    dp_ids = jnp.arange(N_DP, dtype=jnp.int32)
    row_ids = jnp.arange(BROWS, dtype=jnp.int32)
    global_row = dp_ids[:, None, None] * SHARD + within[None, :, None] * BROWS + row_ids[None, None, :]
    alive = global_row < live_rows[source][None, :, None]
    alive = jnp.transpose(alive.reshape(N_DP, N_SECTION, NBLK, BROWS), (1, 0, 2, 3)).reshape(N_SECTION, ROWS, 1)
    generator = jnp.broadcast_to((source < N_GEN).reshape(N_SECTION, 1, NBLK, 1), (N_SECTION, N_DP, NBLK, BROWS))
    generator = generator.reshape(N_SECTION, ROWS, 1)
    updated, first, second, averaged = adam_update(params, moment1, moment2, ema, homed, alive, generator)
    rounded = updated.astype(jnp.bfloat16).reshape(N_SECTION, N_DP, NBLK, BROWS, 128)
    rounded = jnp.transpose(rounded, (1, 0, 2, 3, 4)).reshape(N_DP, N_SECTION * NBLK, BROWS, 128)
    back = rounded[:, position].reshape(N_DP, N_SECTION, NBLK, BROWS, 128)
    weights = jnp.transpose(back, (1, 0, 2, 3, 4)).reshape(N_SECTION, K, C)
    return (updated, first, second, averaged, weights)
```

```python
import jax
import jax.numpy as jnp
from jax import lax
from jax.experimental import pallas as pl
from jax.experimental.pallas import tpu as pltpu
from jax.sharding import PartitionSpec as P

N_GEN = 2
STEP = 100
MESH = pl.DeviceIdType.MESH
BF16, F32 = jnp.bfloat16, jnp.float32

X, Z, Y = 4, 8, 4
LANES = 128
HALF = 72
PIECE = 2 * HALF
BLOCKS = 9
OFFSETS = (2, 1, 3, 0)

S_CORE = 0
S_A1 = S_CORE + 4
S_B1 = S_A1 + 3
S_A2 = S_B1 + 7
S_B2 = S_A2 + 7
S_G = S_B2 + 3
S_H = S_G + 7
S_WA1 = S_H + 7
S_WB1 = S_WA1 + 7
S_WA2 = S_WB1 + 3
S_WB2 = S_WA2 + 3
S_WC = S_WB2 + 7
N_REMOTE = S_WC + 12

L_ACTS = 0
L_COT = L_ACTS + 4
L_STATE = L_COT + 2
L_NEW = L_STATE + 4
L_OUT = L_NEW + 4
N_LOCAL = L_OUT + 24


def kernel(
    acts, cot, params, moment1, moment2, ema, live_rows, home,
    new_params, new_moment1, new_moment2, new_ema, weights,
    acts_buf, cot_buf, own, core_out, core_in,
    a1_out, a1_in, b1_out, b1_in, acc_a, acc_b, a2_out, a2_in, b2_out, b2_in,
    g_out, g_in, g_all, state, fresh, h_all, h_out, h_in, w_all, w_mine, gathered,
    position, order, send_sems, recv_sems, local_sems,
):
    dp = lax.axis_index("dp")
    y = lax.axis_index("section")
    c = lax.rem(dp, 2)
    z = lax.rem(lax.div(dp, 2), Z)
    x = lax.div(dp, 2 * Z)
    sign = 1 - 2 * c

    def xi(k):
        return lax.rem(x + sign * k + 2 * X, X)

    def zi(k):
        return lax.rem(z + sign * k + 2 * Z, Z)

    def at(xx, zz, cc, yy):
        return ((xx * Z + zz) * 2 + cc, yy)

    x_next, x_last = at(xi(1), z, c, y), at(xi(-1), z, c, y)
    z_next, z_last = at(x, zi(1), c, y), at(x, zi(-1), c, y)
    partner = at(x, z, 1 - c, y)
    others = []
    for dy in range(Y):
        for dc in range(2):
            if dy or dc:
                others.append((lax.rem(c + dc, 2), lax.rem(y + dy, Y)))

    barrier = pltpu.get_barrier_semaphore()
    greeted = [x_next, x_last, z_next, z_last] + [at(x, z, cc, yy) for cc, yy in others]
    for device in greeted:
        pl.semaphore_signal(barrier, inc=1, device_id=device, device_id_type=MESH)

    pending = []

    def local(src, dst, index):
        copy = pltpu.make_async_copy(src, dst, local_sems.at[index])
        copy.start()
        return copy

    def send(src, dst, device, index):
        copy = pltpu.make_async_remote_copy(
            src_ref=src, dst_ref=dst, send_sem=send_sems.at[index], recv_sem=recv_sems.at[index],
            device_id=device, device_id_type=MESH,
        )
        copy.start()
        pending.append(copy)
        return copy

    width = Z * PIECE
    cot_copies = []
    for half in range(2):
        column = pl.multiple_of(256 * lax.rem(c + half, 2), 256)
        cot_copies.append(
            local(cot.at[:, pl.ds(column, 256)], cot_buf.at[:, pl.ds(256 * half, 256)], L_COT + half)
        )
    for t, offset in enumerate(OFFSETS):
        column = pl.multiple_of(width * lax.rem(x + offset, X), LANES)
        local(acts.at[:, pl.ds(column, width)], acts_buf.at[t], L_ACTS + t)
    state_copies = [
        local(ref, state.at[n], L_STATE + n) for n, ref in enumerate((params, moment1, moment2, ema))
    ]

    def section_row(s, carry):
        def block_entry(b, carry):
            counts, kept = carry[:Y], carry[Y:]
            keeper = home[s, b]
            rank = jnp.int32(0)
            for n in range(Y):
                rank = jnp.where(keeper == n, counts[n], rank)
            place = keeper * BLOCKS + rank
            position[s * BLOCKS + b] = place
            counts = tuple(counts[n] + jnp.where(keeper == n, 1, 0) for n in range(Y))
            here = place - y * BLOCKS
            kept = tuple(jnp.where(here == n, s * BLOCKS + b, kept[n]) for n in range(BLOCKS))
            return counts + kept

        return lax.fori_loop(0, BLOCKS, block_entry, carry)

    table = lax.fori_loop(0, Y, section_row, (jnp.int32(0),) * (Y + BLOCKS))
    for n in range(BLOCKS):
        order[n] = table[Y + n]

    pl.semaphore_wait(barrier, len(greeted))

    for copy in cot_copies:
        copy.wait()

    def core_copy(t):
        return pltpu.make_async_remote_copy(
            src_ref=core_out.at[t], dst_ref=core_in.at[t],
            send_sem=send_sems.at[S_CORE + t], recv_sem=recv_sems.at[S_CORE + t],
            device_id=partner, device_id_type=MESH,
        )

    @pl.loop(0, X)
    def _(t):
        pltpu.make_async_copy(
            acts.at[:, pl.ds(0, width)], acts_buf.at[t], local_sems.at[L_ACTS + t]
        ).wait()
        product = lax.dot_general(
            acts_buf[t], cot_buf[...], (((0,), (0,)), ((), ())), preferred_element_type=F32
        )
        for h in range(2):
            own[t, h] = product[:, LANES * h : LANES * (h + 1)].reshape(Z, PIECE, LANES)
            other = product[:, 256 + LANES * h : 256 + LANES * (h + 1)]
            core_out[t, h] = other.reshape(Z, PIECE, LANES).astype(BF16)
        core_copy(t).start()

    pending += [core_copy(t) for t in range(X)]

    plus, minus = 1 + c, 2 - c

    def block_a(t):
        return own[t, 0] + core_in[t, 0].astype(F32)

    def block_b(zz):
        return own[:, 1, zz] + core_in[:, 1, zz].astype(F32)

    def give(value, out, into, slot, device, base):
        out[slot] = value.astype(BF16)
        return send(out.at[slot], into.at[slot], device, base + slot)

    def taken(copy, into, slot):
        copy.wait_recv()
        return into[slot].astype(F32)

    core_copy(0).wait_recv()
    a1, b1, a2, b2 = {}, {}, {}, {}
    a1[0] = give(block_a(0), a1_out, a1_in, 0, x_next, S_A1)
    for t in range(1, X):
        core_copy(t).wait_recv()
    b1[0] = give(block_b(zi(4)), b1_out, b1_in, 0, z_next, S_B1)
    b1[4] = give(block_b(zi(-3)), b1_out, b1_in, 4, z_last, S_B1)
    a1[2] = give(block_a(minus), a1_out, a1_in, 2, x_last, S_A1)
    b1[1] = give(block_b(zi(3)) + taken(b1[0], b1_in, 0), b1_out, b1_in, 1, z_next, S_B1)
    b1[5] = give(block_b(zi(-2)) + taken(b1[4], b1_in, 4), b1_out, b1_in, 5, z_last, S_B1)
    a1[1] = give(block_a(plus) + taken(a1[0], a1_in, 0), a1_out, a1_in, 1, x_next, S_A1)
    b1[2] = give(block_b(zi(2)) + taken(b1[1], b1_in, 1), b1_out, b1_in, 2, z_next, S_B1)
    b1[6] = give(block_b(zi(-1)) + taken(b1[5], b1_in, 5), b1_out, b1_in, 6, z_last, S_B1)
    b1[3] = give(block_b(zi(1)) + taken(b1[2], b1_in, 2), b1_out, b1_in, 3, z_next, S_B1)

    acc_a[...] = block_a(3) + taken(a1[2], a1_in, 2) + taken(a1[1], a1_in, 1)
    a2[0] = give(acc_a[zi(4)], a2_out, a2_in, 0, z_next, S_A2)
    a2[4] = give(acc_a[zi(-3)], a2_out, a2_in, 4, z_last, S_A2)
    acc_b[...] = block_b(z) + taken(b1[6], b1_in, 6) + taken(b1[3], b1_in, 3)
    b2[0] = give(acc_b[0], b2_out, b2_in, 0, x_next, S_B2)
    b2[2] = give(acc_b[minus], b2_out, b2_in, 2, x_last, S_B2)
    a2[1] = give(acc_a[zi(3)] + taken(a2[0], a2_in, 0), a2_out, a2_in, 1, z_next, S_A2)
    a2[5] = give(acc_a[zi(-2)] + taken(a2[4], a2_in, 4), a2_out, a2_in, 5, z_last, S_A2)
    b2[1] = give(acc_b[plus] + taken(b2[0], b2_in, 0), b2_out, b2_in, 1, x_next, S_B2)
    a2[2] = give(acc_a[zi(2)] + taken(a2[1], a2_in, 1), a2_out, a2_in, 2, z_next, S_A2)
    a2[6] = give(acc_a[zi(-1)] + taken(a2[5], a2_in, 5), a2_out, a2_in, 6, z_last, S_A2)
    a2[3] = give(acc_a[zi(1)] + taken(a2[2], a2_in, 2), a2_out, a2_in, 3, z_next, S_A2)
    sum_b = acc_b[3] + taken(b2[2], b2_in, 2) + taken(b2[1], b2_in, 1)
    sum_a = acc_a[z] + taken(a2[6], a2_in, 6) + taken(a2[3], a2_in, 3)

    mine = 2 * y + c

    def spread(out, into, base):
        into[mine] = out[c]
        copies = []
        for n, (cc, yy) in enumerate(others):
            copies.append(send(out.at[cc], into.at[mine], at(x, z, cc, yy), base + n))
        for copy in copies:
            copy.wait_recv()

    for cc in range(2):
        rows = slice(HALF * cc, HALF * (cc + 1))
        g_out[cc] = jnp.concatenate([sum_a[rows], sum_b[rows]], axis=0).astype(BF16)
    spread(g_out, g_in, S_G)
    for s in range(Y):
        for cc in range(2):
            value = g_in[2 * s + cc].astype(F32)
            for jj in range(2):
                g_all[2 * cc + jj, BLOCKS * s : BLOCKS * (s + 1)] = value[HALF * jj : HALF * (jj + 1)].reshape(
                    BLOCKS, 8, LANES
                )

    for copy in state_copies:
        copy.wait()
    corr_one = 1.0 - 0.9**STEP
    corr_two = 1.0 - 0.99**STEP

    @pl.loop(0, BLOCKS)
    def _(i):
        f = order[i]
        s = lax.div(f, BLOCKS)
        b = f - s * BLOCKS
        limit = live_rows[s] - (dp * (4 * HALF) + b * 32)
        tile = lax.broadcasted_iota(jnp.int32, (8, LANES), 0)
        generator = tile * 0 + s < N_GEN
        for j in range(4):
            rows = pl.ds(i * 32 + j, 8, stride=4)
            grads = g_all[j, f]
            alive = tile * 4 + j < limit
            p, m1, m2, average = (state[n, rows, :] for n in range(4))
            first = jnp.where(alive, 0.9 * m1 + 0.1 * grads, m1)
            second = jnp.where(alive, 0.99 * m2 + 0.01 * grads * grads, m2)
            stepped = p - 0.0025 * (first / corr_one) / (jnp.sqrt(second / corr_two) + 1e-08)
            updated = jnp.where(alive, stepped, p)
            averaged = jnp.where(generator, 0.995 * average + 0.005 * updated, average)
            for n, value in enumerate((updated, first, second, averaged)):
                fresh[n, rows, :] = value
            h_all[j, pl.ds(pl.multiple_of(i * 8, 8), 8), :] = updated

    for cc in range(2):
        h_out[cc] = h_all[2 * cc : 2 * cc + 2].reshape(PIECE, LANES).astype(BF16)
    spread(h_out, h_in, S_H)
    fresh_copies = [
        local(fresh.at[n], ref, L_NEW + n)
        for n, ref in enumerate((new_params, new_moment1, new_moment2, new_ema))
    ]
    for s in range(Y):
        for cc in range(2):
            value = h_in[2 * s + cc].astype(F32)
            for jj in range(2):
                w_all[jj, cc, BLOCKS * s : BLOCKS * (s + 1)] = value[HALF * jj : HALF * (jj + 1)].reshape(
                    BLOCKS, 8, LANES
                )

    @pl.loop(0, BLOCKS)
    def _(b):
        place = position[y * BLOCKS + b]
        for cc in range(2):
            for jj in range(2):
                w_mine[jj, pl.ds(pl.multiple_of(HALF * cc + b * 8, 8), 8), :] = w_all[jj, cc, place]

    ja, jb = 2 * c, 2 * c + 1
    gathered[ja, x, z] = w_mine[0].astype(BF16)
    gathered[jb, x, z] = w_mine[1].astype(BF16)
    finished = []

    def columns(j):
        return pl.ds(pl.multiple_of(j * LANES, LANES), LANES)

    def store_x(j, xx, index):
        finished.append(local(gathered.at[j, xx], weights.at[xx, :, :, columns(j)], L_OUT + index))

    def store_z(j, zz, index):
        finished.append(local(gathered.at[j, :, zz], weights.at[:, zz, :, columns(j)], L_OUT + index))

    crossing = {}

    def ready_x(xx, index):
        ref = gathered.at[ja, xx]
        crossing[index] = send(ref, ref, partner, S_WC + index)
        store_x(ja, xx, index)

    def ready_z(zz, index):
        ref = gathered.at[jb, :, zz]
        crossing[4 + index] = send(ref, ref, partner, S_WC + 4 + index)
        store_z(jb, zz, 4 + index)

    def pass_on(ref, device, index):
        return send(ref, ref, device, index)

    def chunk_a(k):
        return gathered.at[ja, x, zi(k)]

    def chunk_b(k):
        return gathered.at[jb, xi(k), z]

    def row_a(k):
        return gathered.at[ja, xi(k)]

    def row_b(k):
        return gathered.at[jb, :, zi(k)]

    wa1 = {0: pass_on(chunk_a(0), z_next, S_WA1), 4: pass_on(chunk_a(0), z_last, S_WA1 + 4)}
    wb1 = {0: pass_on(chunk_b(0), x_next, S_WB1), 2: pass_on(chunk_b(0), x_last, S_WB1 + 2)}
    wb1[0].wait_recv()
    wb1[1] = pass_on(chunk_b(-1), x_next, S_WB1 + 1)
    for k in range(1, 4):
        wa1[k - 1].wait_recv()
        wa1[k] = pass_on(chunk_a(-k), z_next, S_WA1 + k)
        if k < 3:
            wa1[k + 3].wait_recv()
            wa1[k + 4] = pass_on(chunk_a(k), z_last, S_WA1 + 4 + k)
    wb1[2].wait_recv()
    wb1[1].wait_recv()
    wb2 = {0: pass_on(row_b(0), z_next, S_WB2), 4: pass_on(row_b(0), z_last, S_WB2 + 4)}
    ready_z(z, 0)
    wa1[6].wait_recv()
    wa1[3].wait_recv()
    wa2 = {0: pass_on(row_a(0), x_next, S_WA2), 2: pass_on(row_a(0), x_last, S_WA2 + 2)}
    ready_x(x, 0)
    for k in range(1, 4):
        wb2[k - 1].wait_recv()
        wb2[k] = pass_on(row_b(-k), z_next, S_WB2 + k)
        ready_z(zi(-k), 2 * k - 1)
        wb2[k + 3].wait_recv()
        if k < 3:
            wb2[k + 4] = pass_on(row_b(k), z_last, S_WB2 + 4 + k)
        ready_z(zi(k), 2 * k)
        if k == 2:
            wa2[0].wait_recv()
            wa2[1] = pass_on(row_a(-1), x_next, S_WA2 + 1)
            ready_x(xi(-1), 1)
            wa2[2].wait_recv()
            ready_x(xi(1), 2)
    wb2[3].wait_recv()
    ready_z(zi(-4), 7)
    wa2[1].wait_recv()
    ready_x(xi(-2), 3)

    qa, qb = 2 * (1 - c), 2 * (1 - c) + 1
    crossing[4].wait_recv()
    store_z(qb, z, 16)
    crossing[0].wait_recv()
    store_x(qa, x, 12)
    for k in range(1, 4):
        crossing[4 + 2 * k - 1].wait_recv()
        store_z(qb, zi(k), 16 + 2 * k - 1)
        crossing[4 + 2 * k].wait_recv()
        store_z(qb, zi(-k), 16 + 2 * k)
        if k == 2:
            crossing[1].wait_recv()
            store_x(qa, xi(1), 13)
            crossing[2].wait_recv()
            store_x(qa, xi(-1), 14)
    crossing[11].wait_recv()
    store_z(qb, zi(4), 23)
    crossing[3].wait_recv()
    store_x(qa, xi(2), 15)

    for copy in fresh_copies + finished:
        copy.wait()
    for copy in pending:
        copy.wait_send()


def body(acts, grad_out, params, moment1, moment2, ema, live_rows, home):
    tokens = acts.shape[1]
    rows = (4 * HALF, LANES)
    any_space = pl.BlockSpec(memory_space=pl.ANY)
    smem = pl.BlockSpec(memory_space=pltpu.SMEM)
    plane = (Z, PIECE, LANES)
    column = (X, PIECE, LANES)
    chunk = (PIECE, LANES)
    outs = pl.pallas_call(
        kernel,
        out_shape=[jax.ShapeDtypeStruct(rows, F32)] * 4
        + [jax.ShapeDtypeStruct((X, Z, PIECE, 4 * LANES), BF16)],
        in_specs=[any_space] * 6 + [smem] * 2,
        out_specs=[any_space] * 5,
        scratch_shapes=[
            pltpu.VMEM((X, tokens, Z * PIECE), BF16),
            pltpu.VMEM((tokens, 4 * LANES), BF16),
            pltpu.VMEM((X, 2) + plane, F32),
            pltpu.VMEM((X, 2) + plane, BF16),
            pltpu.VMEM((X, 2) + plane, BF16),
            pltpu.VMEM((3,) + plane, BF16),
            pltpu.VMEM((3,) + plane, BF16),
            pltpu.VMEM((7,) + column, BF16),
            pltpu.VMEM((7,) + column, BF16),
            pltpu.VMEM(plane, F32),
            pltpu.VMEM(column, F32),
            pltpu.VMEM((7,) + chunk, BF16),
            pltpu.VMEM((7,) + chunk, BF16),
            pltpu.VMEM((3,) + chunk, BF16),
            pltpu.VMEM((3,) + chunk, BF16),
            pltpu.VMEM((2,) + chunk, BF16),
            pltpu.VMEM((2 * Y,) + chunk, BF16),
            pltpu.VMEM((4, Y * BLOCKS, 8, LANES), F32),
            pltpu.VMEM((4,) + rows, F32),
            pltpu.VMEM((4,) + rows, F32),
            pltpu.VMEM((4, HALF, LANES), F32),
            pltpu.VMEM((2,) + chunk, BF16),
            pltpu.VMEM((2 * Y,) + chunk, BF16),
            pltpu.VMEM((2, 2, Y * BLOCKS, 8, LANES), F32),
            pltpu.VMEM((2,) + chunk, F32),
            pltpu.VMEM((4, X) + plane, BF16),
            pltpu.SMEM((Y * BLOCKS,), jnp.int32),
            pltpu.SMEM((BLOCKS,), jnp.int32),
            pltpu.SemaphoreType.DMA((N_REMOTE,)),
            pltpu.SemaphoreType.DMA((N_REMOTE,)),
            pltpu.SemaphoreType.DMA((N_LOCAL,)),
        ],
        compiler_params=pltpu.CompilerParams(
            collective_id=0, has_side_effects=True, vmem_limit_bytes=56 * 2**20
        ),
    )(acts[0], grad_out[0], params[0], moment1[0], moment2[0], ema[0], live_rows, home)
    updated, first, second, averaged, weights = outs
    return (
        updated[None], first[None], second[None], averaged[None],
        weights.reshape(1, X * Z * PIECE, 4 * LANES),
    )


def solution(mesh):
    split = P("section", "dp", None)
    in_specs = (split,) * 6 + (P(), P())
    out_specs = (split,) * 4 + (P("section", None, None),)
    return jax.shard_map(body, mesh=mesh, in_specs=in_specs, out_specs=out_specs, check_vma=False)
```

```python
import jax
import jax.numpy as jnp
from jax import lax
from jax.experimental import pallas as pl
from jax.experimental.pallas import tpu as pltpu
from jax.sharding import PartitionSpec as P

N_GEN = 2
STEP = 100
MESH = pl.DeviceIdType.MESH
BF16, F32 = jnp.bfloat16, jnp.float32

X, Z, Y = 4, 8, 4
LANES = 128
HALF = 72
PIECE = 2 * HALF
BLOCKS = 9
OFFSETS = (2, 1, 3, 0)

LATENCY, PIECE_US, STEP_US = 2.2, 0.39, 0.12


def in_order(steps):
    left = {}

    def ahead(name):
        if name not in left:
            later = [
                ahead(other) + (LATENCY + PIECE_US if how == "sent" else 0.0)
                for other, (_, needs, _) in steps.items()
                for how, needed in needs
                if needed == name
            ]
            left[name] = steps[name][0] + max(later, default=0.0)
        return left[name]

    for name in steps:
        ahead(name)
    now, link_free, done, arrived, order = 0.0, {}, {}, {}, []
    while len(order) < len(steps):
        ready = []
        for name, (_, needs, _) in steps.items():
            if name in done:
                continue
            times = [(done if how == "done" else arrived).get(needed) for how, needed in needs]
            if None not in times:
                ready.append((max(times, default=0.0), -left[name], name))
        able = [(key, when, name) for when, key, name in ready if when <= now]
        if not able:
            now = min(ready)[0]
            continue
        name = min(able)[2]
        now += steps[name][0]
        done[name] = now
        for link, pieces in steps[name][2].items():
            link_free[link] = max(link_free.get(link, 0.0), now) + PIECE_US * pieces
            arrived[name] = max(arrived.get(name, 0.0), link_free[link] + LATENCY)
        order.append(name)
    return order, now


CHAIN = (4, 3, -3, 2, -2, 1, -1)
ROLES = ("far", "plus", "minus", "mine")


def before(k):
    return None if k in (4, -3) else k + 1 if k > 0 else k - 1


def sum_steps():
    steps = {}
    for t in range(X):
        steps["mul", t] = (1.4, [("done", ("mul", t - 1))] if t else [], {"core%d" % t: 0.5})

    def have(*blocks):
        return [("sent", ("mul", t)) for t in blocks]

    for k in CHAIN + (0,):
        steps["a1", "far", k] = (STEP_US, have(0), {"x": 1})
        steps["a1", "minus", k] = (STEP_US, have(1, 2), {"x": 1})
        steps["a1", "plus", k] = (STEP_US, have(1, 2) + [("sent", ("a1", "far", k))], {"x": 1})
        needs = have(3) + [("sent", ("a1", "plus", k)), ("sent", ("a1", "minus", k))]
        if k == 0:
            needs += [("sent", ("a2", 1)), ("sent", ("a2", -1))]
        elif before(k) is not None:
            needs.append(("sent", ("a2", before(k))))
        steps["a2", k] = (STEP_US, needs, {"z": 1} if k else {})
    for role in ROLES:
        block = {"far": (0,), "plus": (1, 2), "minus": (1, 2), "mine": (3,)}[role]
        for k in CHAIN:
            needs = have(*block)
            if before(k) is not None:
                needs.append(("sent", ("b1", role, before(k))))
            steps["b1", role, k] = (STEP_US, needs, {"z": 1})
        needs = have(*block) + [("sent", ("b1", role, 1)), ("sent", ("b1", role, -1))]
        needs += {
            "far": [], "minus": [], "plus": [("sent", ("b2", "far"))],
            "mine": [("sent", ("b2", "plus")), ("sent", ("b2", "minus"))],
        }[role]
        steps["b2", role] = (STEP_US, needs, {} if role == "mine" else {"x": 1})
    return steps


def gather_steps():
    steps = {}
    places = (0, -1, 1, -2, 2, -3, 3, -4)
    for k in places:
        links = {}
        for i in (0, -1, 1, -2):
            if i == 0:
                needs = [] if k == 0 else [("sent", ("wa", 0, k + 1 if k < 0 else k - 1))]
                links = {"z": (2 if k == 0 else 1 if k in (-1, -2, -3, 1, 2) else 0), "x": 2}
            else:
                needs = [("sent", ("wa", i + 1 if i < 0 else i - 1, k))]
                links = {"x": 1 if i == -1 else 0}
            steps["wa", i, k] = (STEP_US, needs, links)
            if k == 0:
                needs = [] if i == 0 else [("sent", ("wb", i + 1 if i < 0 else i - 1, 0))]
                links = {"x": (2 if i == 0 else 1 if i == -1 else 0), "z": 2}
            else:
                needs = [("sent", ("wb", i, k + 1 if k < 0 else k - 1))]
                links = {"z": 1 if k in (-1, -2, -3, 1, 2) else 0}
            steps["wb", i, k] = (STEP_US, needs, links)
    return steps


def numbered(names, start):
    return {name: start + n for n, name in enumerate(names)}


S_CORE = 0
S_SUM = numbered([name for name in sum_steps() if name[0] != "mul" and name not in (("a2", 0), ("b2", "mine"))], 4)
S_G = 4 + len(S_SUM)
S_H = S_G + 7
S_WAY = numbered(
    [name + (way,) for name in gather_steps() for way in ("z_next", "z_last", "x_next", "x_last")], 0
)
N_SUM = len(S_SUM)

L_ACTS = 0
L_COT = L_ACTS + 4
L_STATE = L_COT + 2
L_NEW = L_STATE + 4
L_OUT = L_NEW + 1
N_LOCAL = L_OUT + 24


def kernel(
    acts, cot, params, moment1, moment2, ema, live_rows, home, new_state, refreshed,
    acts_buf, cot_buf, own, core_out, core_in, sum_out, sum_in,
    g_out, g_in, g_all, state, fresh, h_all, h_out, h_in, w_all, w_mine, gathered,
    position, order, send_sems, recv_sems, way_send, way_recv, local_sems,
):
    dp = lax.axis_index("dp")
    y = lax.axis_index("section")
    c = lax.rem(dp, 2)
    z = lax.rem(lax.div(dp, 2), Z)
    x = lax.div(dp, 2 * Z)
    sign = 1 - 2 * c

    def xi(k):
        return lax.rem(x + sign * k + 2 * X, X)

    def zi(k):
        return lax.rem(z + sign * k + 2 * Z, Z)

    def at(xx, zz, cc, yy):
        return ((xx * Z + zz) * 2 + cc, yy)

    x_next, x_last = at(xi(1), z, c, y), at(xi(-1), z, c, y)
    z_next, z_last = at(x, zi(1), c, y), at(x, zi(-1), c, y)
    partner = at(x, z, 1 - c, y)
    others = []
    for dy in range(Y):
        for dc in range(2):
            if dy or dc:
                others.append((lax.rem(c + dc, 2), lax.rem(y + dy, Y)))

    barrier = pltpu.get_barrier_semaphore()
    greeted = [x_next, x_last, z_next, z_last] + [at(x, z, cc, yy) for cc, yy in others]
    for device in greeted:
        pl.semaphore_signal(barrier, inc=1, device_id=device, device_id_type=MESH)

    pending = []

    def local(src, dst, index):
        copy = pltpu.make_async_copy(src, dst, local_sems.at[index])
        copy.start()
        return copy

    def send(src, dst, device, sent, arrived):
        copy = pltpu.make_async_remote_copy(
            src_ref=src, dst_ref=dst, send_sem=sent, recv_sem=arrived,
            device_id=device, device_id_type=MESH,
        )
        copy.start()
        pending.append(copy)
        return copy

    width = Z * PIECE
    cot_copies = []
    for half in range(2):
        column = pl.multiple_of(256 * lax.rem(c + half, 2), 256)
        cot_copies.append(
            local(cot.at[:, pl.ds(column, 256)], cot_buf.at[:, pl.ds(256 * half, 256)], L_COT + half)
        )
    for t, offset in enumerate(OFFSETS):
        column = pl.multiple_of(width * lax.rem(x + offset, X), LANES)
        local(acts.at[:, pl.ds(column, width)], acts_buf.at[t], L_ACTS + t)
    state_copies = [
        local(ref, state.at[n], L_STATE + n) for n, ref in enumerate((params, moment1, moment2, ema))
    ]

    def section_row(s, carry):
        def block_entry(b, carry):
            counts, kept = carry[:Y], carry[Y:]
            keeper = home[s, b]
            rank = jnp.int32(0)
            for n in range(Y):
                rank = jnp.where(keeper == n, counts[n], rank)
            place = keeper * BLOCKS + rank
            position[s * BLOCKS + b] = place
            counts = tuple(counts[n] + jnp.where(keeper == n, 1, 0) for n in range(Y))
            here = place - y * BLOCKS
            kept = tuple(jnp.where(here == n, s * BLOCKS + b, kept[n]) for n in range(BLOCKS))
            return counts + kept

        return lax.fori_loop(0, BLOCKS, block_entry, carry)

    table = lax.fori_loop(0, Y, section_row, (jnp.int32(0),) * (Y + BLOCKS))
    for n in range(BLOCKS):
        order[n] = table[Y + n]

    pl.semaphore_wait(barrier, len(greeted))

    for copy in cot_copies:
        copy.wait()

    def core_copy(t):
        return pltpu.make_async_remote_copy(
            src_ref=core_out.at[t], dst_ref=core_in.at[t],
            send_sem=send_sems.at[S_CORE + t], recv_sem=recv_sems.at[S_CORE + t],
            device_id=partner, device_id_type=MESH,
        )

    def multiply(t):
        pltpu.make_async_copy(
            acts.at[:, pl.ds(0, width)], acts_buf.at[t], local_sems.at[L_ACTS + t]
        ).wait()
        product = lax.dot_general(
            acts_buf[t], cot_buf[...], (((0,), (0,)), ((), ())), preferred_element_type=F32
        )
        for h in range(2):
            own[t, h] = product[:, LANES * h : LANES * (h + 1)].reshape(Z, PIECE, LANES)
            other = product[:, 256 + LANES * h : 256 + LANES * (h + 1)]
            core_out[t, h] = other.reshape(Z, PIECE, LANES).astype(BF16)
        copy = core_copy(t)
        copy.start()
        pending.append(copy)

    here = {"far": 0, "plus": 1 + c, "minus": 2 - c, "mine": 3}
    needed = {"far": (0,), "plus": (1, 2), "minus": (1, 2), "mine": (3,)}
    crossed, moving = set(), {}

    def block(h, role, k):
        for t in needed[role]:
            if t not in crossed:
                core_copy(t).wait_recv()
                crossed.add(t)
        return own[here[role], h, zi(k)] + core_in[here[role], h, zi(k)].astype(F32)

    def taken(name):
        moving[name].wait_recv()
        return sum_in[S_SUM[name] - 4].astype(F32)

    def give(name, value, device):
        slot = S_SUM[name] - 4
        sum_out[slot] = value.astype(BF16)
        moving[name] = send(
            sum_out.at[slot], sum_in.at[slot], device, send_sems.at[S_SUM[name]], recv_sems.at[S_SUM[name]]
        )

    def along_x(role):
        return x_last if role == "minus" else x_next

    def along_z(k):
        return z_next if k > 0 else z_last

    for name in in_order(sum_steps())[0]:
        if name[0] == "mul":
            multiply(name[1])
        elif name[0] == "a1":
            _, role, k = name
            value = block(0, role, k)
            if role == "plus":
                value = value + taken(("a1", "far", k))
            give(name, value, along_x(role))
        elif name[0] == "a2":
            k = name[1]
            value = block(0, "mine", k) + taken(("a1", "minus", k)) + taken(("a1", "plus", k))
            for earlier in (1, -1) if k == 0 else () if before(k) is None else (before(k),):
                value = value + taken(("a2", earlier))
            if k == 0:
                sum_a = value
            else:
                give(name, value, along_z(k))
        elif name[0] == "b1":
            _, role, k = name
            value = block(1, role, k)
            if before(k) is not None:
                value = value + taken(("b1", role, before(k)))
            give(name, value, along_z(k))
        else:
            role = name[1]
            value = block(1, role, 0) + taken(("b1", role, 1)) + taken(("b1", role, -1))
            for earlier in {"plus": ("far",), "mine": ("plus", "minus")}.get(role, ()):
                value = value + taken(("b2", earlier))
            if role == "mine":
                sum_b = value
            else:
                give(name, value, along_x(role))

    mine = 2 * y + c

    def spread(out, into, base):
        into[mine] = out[c]
        copies = []
        for n, (cc, yy) in enumerate(others):
            copies.append(
                send(
                    out.at[cc], into.at[mine], at(x, z, cc, yy), send_sems.at[base + n], recv_sems.at[base + n]
                )
            )
        for copy in copies:
            copy.wait_recv()

    for cc in range(2):
        rows = slice(HALF * cc, HALF * (cc + 1))
        g_out[cc] = jnp.concatenate([sum_a[rows], sum_b[rows]], axis=0).astype(BF16)
    spread(g_out, g_in, S_G)
    for s in range(Y):
        for cc in range(2):
            value = g_in[2 * s + cc].astype(F32)
            for jj in range(2):
                g_all[2 * cc + jj, BLOCKS * s : BLOCKS * (s + 1)] = value[HALF * jj : HALF * (jj + 1)].reshape(
                    BLOCKS, 8, LANES
                )

    for copy in state_copies:
        copy.wait()
    corr_one = 1.0 - 0.9**STEP
    corr_two = 1.0 - 0.99**STEP

    @pl.loop(0, BLOCKS)
    def _(i):
        f = order[i]
        s = lax.div(f, BLOCKS)
        b = f - s * BLOCKS
        limit = live_rows[s] - (dp * (4 * HALF) + b * 32)
        tile = lax.broadcasted_iota(jnp.int32, (8, LANES), 0)
        generator = tile * 0 + s < N_GEN
        for j in range(4):
            rows = pl.ds(i * 32 + j, 8, stride=4)
            grads = g_all[j, f]
            alive = tile * 4 + j < limit
            p, m1, m2, average = (state[n, rows, :] for n in range(4))
            first = jnp.where(alive, 0.9 * m1 + 0.1 * grads, m1)
            second = jnp.where(alive, 0.99 * m2 + 0.01 * grads * grads, m2)
            stepped = p - 0.0025 * (first / corr_one) / (jnp.sqrt(second / corr_two) + 1e-08)
            updated = jnp.where(alive, stepped, p)
            averaged = jnp.where(generator, 0.995 * average + 0.005 * updated, average)
            for n, value in enumerate((updated, first, second, averaged)):
                fresh[n, rows, :] = value
            h_all[j, pl.ds(pl.multiple_of(i * 8, 8), 8), :] = updated

    for cc in range(2):
        h_out[cc] = h_all[2 * cc : 2 * cc + 2].reshape(PIECE, LANES).astype(BF16)
    spread(h_out, h_in, S_H)
    fresh_copy = local(fresh, new_state, L_NEW)
    for s in range(Y):
        for cc in range(2):
            value = h_in[2 * s + cc].astype(F32)
            for jj in range(2):
                w_all[jj, cc, BLOCKS * s : BLOCKS * (s + 1)] = value[HALF * jj : HALF * (jj + 1)].reshape(
                    BLOCKS, 8, LANES
                )

    @pl.loop(0, BLOCKS)
    def _(b):
        place = position[y * BLOCKS + b]
        for cc in range(2):
            for jj in range(2):
                w_mine[jj, pl.ds(pl.multiple_of(HALF * cc + b * 8, 8), 8), :] = w_all[jj, cc, place]

    ja, jb = 2 * c, 2 * c + 1
    gathered[ja, x, z] = w_mine[0].astype(BF16)
    gathered[jb, x, z] = w_mine[1].astype(BF16)
    halves = {"wa": ja, "wb": jb}
    ways = {"z_next": z_next, "z_last": z_last, "x_next": x_next, "x_last": x_last}

    def go(name, way):
        _, i, k = name
        ref = gathered.at[halves[name[0]], xi(i), zi(k)]
        number = S_WAY[name + (way,)]
        moving[name + (way,)] = send(ref, ref, ways[way], way_send.at[number], way_recv.at[number])

    def comes(name, axis, i):
        back = i + 1 if i < 0 else i - 1
        at_sender = (name[0], back, name[2]) if axis == "x" else (name[0], name[1], back)
        moving[at_sender + (axis + ("_next" if i < 0 else "_last"),)].wait_recv()

    def onward(axis, i, size):
        if i == 0:
            return [axis + "_next", axis + "_last"]
        if i < 0:
            return [axis + "_next"] if i > -(size // 2) else []
        return [axis + "_last"] if i < size // 2 - 1 else []

    seen, crossing, written = [], {}, []

    def write(j, xx, zz):
        lanes = pl.ds(pl.multiple_of(j * LANES, LANES), LANES)
        if xx is not None:
            source, target = gathered.at[j, xx], refreshed.at[xx, :, :, lanes]
        else:
            source, target = gathered.at[j, :, zz], refreshed.at[:, zz, :, lanes]
        written.append(local(source, target, L_OUT + len(written)))

    def cross(half, i, k):
        number = len(crossing)
        write(halves[half], None if half == "wb" else xi(i), zi(k))
        ref = gathered.at[halves[half], xi(i)] if half == "wa" else gathered.at[halves[half], :, zi(k)]
        crossing[half, i, k] = send(ref, ref, partner, send_sems.at[S_H + 7 + number], recv_sems.at[S_H + 7 + number])

    for name in in_order(gather_steps())[0]:
        half, i, k = name
        first, second = (("z", k, Z), ("x", i, X)) if half == "wa" else (("x", i, X), ("z", k, Z))
        if second[1] != 0:
            comes(name, *second[:2])
            moves = onward(*second)
        else:
            if first[1] != 0:
                comes(name, *first[:2])
            moves = onward(*first) + onward(*second)
        for way in moves:
            go(name, way)
        seen.append(name)
        if half == "wa" and sum(n[:2] == name[:2] for n in seen) == Z:
            cross("wa", i, 0)
        if half == "wb" and sum(n[0] == "wb" and n[2] == k for n in seen) == X:
            cross("wb", 0, k)

    for (half, i, k), copy in crossing.items():
        copy.wait_recv()
        write(2 * (1 - c) + (half == "wb"), None if half == "wb" else xi(-i), zi(-k))
    for copy in written:
        copy.wait()
    fresh_copy.wait()
    for copy in pending:
        copy.wait_send()


def write_out(
    new_state, refreshed, new_params, new_moment1, new_moment2, new_ema, weights, state_buf, buf, in_sems, out_sems
):
    moves = [
        (new_state.at[n], state_buf.at[n], ref)
        for n, ref in enumerate((new_params, new_moment1, new_moment2, new_ema))
    ]
    for xx in range(X):
        for half in range(2):
            part = pl.ds(4 * half, 4)
            moves.append((refreshed.at[xx, part], buf.at[xx, part], weights.at[xx, part]))
    first = [pltpu.make_async_copy(a, b, in_sems.at[n]) for n, (a, b, _) in enumerate(moves)]
    second = [pltpu.make_async_copy(b, d, out_sems.at[n]) for n, (_, b, d) in enumerate(moves)]
    for copy in first:
        copy.start()
    for arrived, copy in zip(first, second):
        arrived.wait()
        copy.start()
    for copy in second:
        copy.wait()


def body(acts, grad_out, params, moment1, moment2, ema, live_rows, home):
    tokens = acts.shape[1]
    rows = (4 * HALF, LANES)
    any_space = pl.BlockSpec(memory_space=pl.ANY)
    smem = pl.BlockSpec(memory_space=pltpu.SMEM)
    plane = (Z, PIECE, LANES)
    chunk = (PIECE, LANES)
    outs = pl.pallas_call(
        kernel,
        out_shape=[
            jax.ShapeDtypeStruct((4,) + rows, F32),
            jax.ShapeDtypeStruct((X, Z, PIECE, 4 * LANES), BF16),
        ],
        in_specs=[any_space] * 6 + [smem] * 2,
        out_specs=[any_space] * 2,
        scratch_shapes=[
            pltpu.VMEM((X, tokens, Z * PIECE), BF16),
            pltpu.VMEM((tokens, 4 * LANES), BF16),
            pltpu.VMEM((X, 2) + plane, F32),
            pltpu.VMEM((X, 2) + plane, BF16),
            pltpu.VMEM((X, 2) + plane, BF16),
            pltpu.VMEM((N_SUM,) + chunk, BF16),
            pltpu.VMEM((N_SUM,) + chunk, BF16),
            pltpu.VMEM((2,) + chunk, BF16),
            pltpu.VMEM((2 * Y,) + chunk, BF16),
            pltpu.VMEM((4, Y * BLOCKS, 8, LANES), F32),
            pltpu.VMEM((4,) + rows, F32),
            pltpu.VMEM((4,) + rows, F32),
            pltpu.VMEM((4, HALF, LANES), F32),
            pltpu.VMEM((2,) + chunk, BF16),
            pltpu.VMEM((2 * Y,) + chunk, BF16),
            pltpu.VMEM((2, 2, Y * BLOCKS, 8, LANES), F32),
            pltpu.VMEM((2,) + chunk, F32),
            pltpu.VMEM((4, X) + plane, BF16),
            pltpu.SMEM((Y * BLOCKS,), jnp.int32),
            pltpu.SMEM((BLOCKS,), jnp.int32),
            pltpu.SemaphoreType.DMA((S_H + 19,)),
            pltpu.SemaphoreType.DMA((S_H + 19,)),
            pltpu.SemaphoreType.DMA((len(S_WAY),)),
            pltpu.SemaphoreType.DMA((len(S_WAY),)),
            pltpu.SemaphoreType.DMA((N_LOCAL,)),
        ],
        compiler_params=pltpu.CompilerParams(
            collective_id=0, has_side_effects=True, vmem_limit_bytes=56 * 2**20
        ),
    )(acts[0], grad_out[0], params[0], moment1[0], moment2[0], ema[0], live_rows, home)
    updated, first, second, averaged, weights = pl.pallas_call(
        write_out,
        out_shape=[jax.ShapeDtypeStruct(rows, F32)] * 4
        + [jax.ShapeDtypeStruct((X, Z, PIECE, 4 * LANES), BF16)],
        in_specs=[any_space] * 2,
        out_specs=[any_space] * 5,
        scratch_shapes=[
            pltpu.VMEM((4,) + rows, F32),
            pltpu.VMEM((X, Z, PIECE, 4 * LANES), BF16),
            pltpu.SemaphoreType.DMA((4 + 2 * X,)),
            pltpu.SemaphoreType.DMA((4 + 2 * X,)),
        ],
        compiler_params=pltpu.CompilerParams(vmem_limit_bytes=56 * 2**20),
    )(*outs)
    return (
        updated[None], first[None], second[None], averaged[None],
        weights.reshape(1, X * Z * PIECE, 4 * LANES),
    )


def solution(mesh):
    split = P("section", "dp", None)
    in_specs = (split,) * 6 + (P(), P())
    out_specs = (split,) * 4 + (P("section", None, None),)
    return jax.shard_map(body, mesh=mesh, in_specs=in_specs, out_specs=out_specs, check_vma=False)
```

```python
import jax
import jax.numpy as jnp
from jax import lax
from jax.experimental import pallas as pl
from jax.experimental.pallas import tpu as pltpu
from jax.sharding import PartitionSpec as P

N_GEN = 2
STEP = 100
MESH = pl.DeviceIdType.MESH
BF16, F32 = jnp.bfloat16, jnp.float32

X, Z, Y = 4, 8, 4
LANES = 128
HALF = 72
PIECE = 2 * HALF
BLOCKS = 9
OFFSETS = (2, 1, 3, 0)

LATENCY, PIECE_US, STEP_US = 2.2, 0.39, 0.12


def in_order(steps):
    left = {}

    def ahead(name):
        if name not in left:
            later = [
                ahead(other) + (LATENCY + PIECE_US if how == "sent" else 0.0)
                for other, (_, needs, _) in steps.items()
                for how, needed in needs
                if needed == name
            ]
            left[name] = steps[name][0] + max(later, default=0.0)
        return left[name]

    for name in steps:
        ahead(name)
    now, link_free, done, arrived, order = 0.0, {}, {}, {}, []
    while len(order) < len(steps):
        ready = []
        for name, (_, needs, _) in steps.items():
            if name in done:
                continue
            times = [(done if how == "done" else arrived).get(needed) for how, needed in needs]
            if None not in times:
                ready.append((max(times, default=0.0), -left[name], name))
        able = [(key, when, name) for when, key, name in ready if when <= now]
        if not able:
            now = min(ready)[0]
            continue
        name = min(able)[2]
        now += steps[name][0]
        done[name] = now
        for link, pieces in steps[name][2].items():
            link_free[link] = max(link_free.get(link, 0.0), now) + PIECE_US * pieces
            arrived[name] = max(arrived.get(name, 0.0), link_free[link] + LATENCY)
        order.append(name)
    return order, now


CHAIN = (4, 3, -3, 2, -2, 1, -1)
ROLES = ("far", "plus", "minus", "mine")


def before(k):
    return None if k in (4, -3) else k + 1 if k > 0 else k - 1


def sum_steps():
    steps = {}
    for t in range(X):
        steps["mul", t] = (1.4, [("done", ("mul", t - 1))] if t else [], {"core%d" % t: 0.5})

    def have(*blocks):
        return [("sent", ("mul", t)) for t in blocks]

    for k in CHAIN + (0,):
        steps["a1", "far", k] = (STEP_US, have(0), {"x": 1})
        steps["a1", "minus", k] = (STEP_US, have(1, 2), {"x": 1})
        steps["a1", "plus", k] = (STEP_US, have(1, 2) + [("sent", ("a1", "far", k))], {"x": 1})
        needs = have(3) + [("sent", ("a1", "plus", k)), ("sent", ("a1", "minus", k))]
        if k == 0:
            needs += [("sent", ("a2", 1)), ("sent", ("a2", -1))]
        elif before(k) is not None:
            needs.append(("sent", ("a2", before(k))))
        steps["a2", k] = (STEP_US, needs, {"z": 1} if k else {})
    for role in ROLES:
        block = {"far": (0,), "plus": (1, 2), "minus": (1, 2), "mine": (3,)}[role]
        for k in CHAIN:
            needs = have(*block)
            if before(k) is not None:
                needs.append(("sent", ("b1", role, before(k))))
            steps["b1", role, k] = (STEP_US, needs, {"z": 1})
        needs = have(*block) + [("sent", ("b1", role, 1)), ("sent", ("b1", role, -1))]
        needs += {
            "far": [], "minus": [], "plus": [("sent", ("b2", "far"))],
            "mine": [("sent", ("b2", "plus")), ("sent", ("b2", "minus"))],
        }[role]
        steps["b2", role] = (STEP_US, needs, {} if role == "mine" else {"x": 1})
    return steps


def gather_steps():
    steps = {}
    places = (0, -1, 1, -2, 2, -3, 3, -4)
    for k in places:
        links = {}
        for i in (0, -1, 1, -2):
            if i == 0:
                needs = [] if k == 0 else [("sent", ("wa", 0, k + 1 if k < 0 else k - 1))]
                links = {"z": (2 if k == 0 else 1 if k in (-1, -2, -3, 1, 2) else 0), "x": 2}
            else:
                needs = [("sent", ("wa", i + 1 if i < 0 else i - 1, k))]
                links = {"x": 1 if i == -1 else 0}
            steps["wa", i, k] = (STEP_US, needs, links)
            if k == 0:
                needs = [] if i == 0 else [("sent", ("wb", i + 1 if i < 0 else i - 1, 0))]
                links = {"x": (2 if i == 0 else 1 if i == -1 else 0), "z": 2}
            else:
                needs = [("sent", ("wb", i, k + 1 if k < 0 else k - 1))]
                links = {"z": 1 if k in (-1, -2, -3, 1, 2) else 0}
            steps["wb", i, k] = (STEP_US, needs, links)
    return steps


def numbered(names, start):
    return {name: start + n for n, name in enumerate(names)}


def onward(axis, i, size):
    if i == 0:
        return [axis + "_next", axis + "_last"]
    if i < 0:
        return [axis + "_next"] if i > -(size // 2) else []
    return [axis + "_last"] if i < size // 2 - 1 else []


def ways_on(name):
    half, i, k = name
    if half == "wa":
        return (onward("z", k, Z) if i == 0 else []) + onward("x", i, X)
    return (onward("x", i, X) if k == 0 else []) + onward("z", k, Z)


R_CORE = 0
R_SUM = numbered([name for name in sum_steps() if name[0] != "mul" and name not in (("a2", 0), ("b2", "mine"))], 4)
N_SUM = len(R_SUM)
R_G = 4 + N_SUM
R_H = R_G + 7
R_CROSS = R_H + 7
R_WAY = numbered([name + (way,) for name in gather_steps() for way in ways_on(name)], R_CROSS + 12)
N_ARRIVE = R_CROSS + 12 + len(R_WAY)
S_CORE, S_SUM, S_G, S_H, S_WAY, S_ROW, S_COLUMN = range(7)

L_ACTS = 0
L_COT = L_ACTS + 4
L_STATE = L_COT + 2
L_NEW = L_STATE + 4
L_OUT = L_NEW + 1
N_LOCAL = L_OUT + 24


def kernel(
    acts, cot, params, moment1, moment2, ema, live_rows, home, new_state, refreshed,
    acts_buf, cot_buf, own, core_out, core_in, sum_out, sum_in,
    g_out, g_in, g_all, state, fresh, h_all, h_out, h_in, w_all, w_mine, gathered,
    position, order, send_sems, recv_sems, local_sems,
):
    dp = lax.axis_index("dp")
    y = lax.axis_index("section")
    c = lax.rem(dp, 2)
    z = lax.rem(lax.div(dp, 2), Z)
    x = lax.div(dp, 2 * Z)
    sign = 1 - 2 * c

    def xi(k):
        return lax.rem(x + sign * k + 2 * X, X)

    def zi(k):
        return lax.rem(z + sign * k + 2 * Z, Z)

    def at(xx, zz, cc, yy):
        return ((xx * Z + zz) * 2 + cc, yy)

    x_next, x_last = at(xi(1), z, c, y), at(xi(-1), z, c, y)
    z_next, z_last = at(x, zi(1), c, y), at(x, zi(-1), c, y)
    partner = at(x, z, 1 - c, y)
    others = []
    for dy in range(Y):
        for dc in range(2):
            if dy or dc:
                others.append((lax.rem(c + dc, 2), lax.rem(y + dy, Y)))

    barrier = pltpu.get_barrier_semaphore()
    greeted = [x_next, x_last, z_next, z_last] + [at(x, z, cc, yy) for cc, yy in others]
    for device in greeted:
        pl.semaphore_signal(barrier, inc=1, device_id=device, device_id_type=MESH)

    def local(src, dst, index):
        copy = pltpu.make_async_copy(src, dst, local_sems.at[index])
        copy.start()
        return copy

    def send(src, dst, device, group, number):
        copy = pltpu.make_async_remote_copy(
            src_ref=src, dst_ref=dst, send_sem=send_sems.at[group], recv_sem=recv_sems.at[number],
            device_id=device, device_id_type=MESH,
        )
        copy.start()
        return copy

    width = Z * PIECE
    cot_copies = []
    for half in range(2):
        column = pl.multiple_of(256 * lax.rem(c + half, 2), 256)
        cot_copies.append(
            local(cot.at[:, pl.ds(column, 256)], cot_buf.at[:, pl.ds(256 * half, 256)], L_COT + half)
        )
    for t, offset in enumerate(OFFSETS):
        column = pl.multiple_of(width * lax.rem(x + offset, X), LANES)
        local(acts.at[:, pl.ds(column, width)], acts_buf.at[t], L_ACTS + t)
    state_copies = [
        local(ref, state.at[n], L_STATE + n) for n, ref in enumerate((params, moment1, moment2, ema))
    ]

    pl.semaphore_wait(barrier, len(greeted))

    for copy in cot_copies:
        copy.wait()

    def core_copy(t):
        return pltpu.make_async_remote_copy(
            src_ref=core_out.at[t], dst_ref=core_in.at[t],
            send_sem=send_sems.at[S_CORE], recv_sem=recv_sems.at[R_CORE + t],
            device_id=partner, device_id_type=MESH,
        )

    here = {"far": 0, "plus": 1 + c, "minus": 2 - c, "mine": 3}
    needed = {"far": (0,), "plus": (1, 2), "minus": (1, 2), "mine": (3,)}
    crossed, moving = {0}, {}

    def block(h, role, k):
        for t in needed[role]:
            if t not in crossed:
                core_copy(t).wait_recv()
                crossed.add(t)
        return own[here[role], h, zi(k)] + core_in[here[role], h, zi(k)].astype(F32)

    def taken(name):
        moving[name].wait_recv()
        return sum_in[R_SUM[name] - 4].astype(F32)

    def piece_copy(name, device):
        slot = R_SUM[name] - 4
        return pltpu.make_async_remote_copy(
            src_ref=sum_out.at[slot], dst_ref=sum_in.at[slot],
            send_sem=send_sems.at[S_SUM], recv_sem=recv_sems.at[R_SUM[name]],
            device_id=device, device_id_type=MESH,
        )

    def remember(name, device):
        moving[name] = piece_copy(name, device)

    def give(name, value, device):
        sum_out[R_SUM[name] - 4] = value.astype(BF16)
        piece_copy(name, device).start()
        remember(name, device)

    def along_x(role):
        return x_last if role == "minus" else x_next

    def along_z(k):
        return z_next if k > 0 else z_last

    early = [("a1", "far", k) for k in CHAIN + (0,)] + [("b1", "far", 4), ("b1", "far", -3)]

    @pl.loop(0, X)
    def _(t):
        pltpu.make_async_copy(
            acts.at[:, pl.ds(0, width)], acts_buf.at[t], local_sems.at[L_ACTS + t]
        ).wait()
        product = lax.dot_general(
            acts_buf[t], cot_buf[...], (((0,), (0,)), ((), ())), preferred_element_type=F32
        )
        for h in range(2):
            own[t, h] = product[:, LANES * h : LANES * (h + 1)].reshape(Z, PIECE, LANES)
            other = product[:, 256 + LANES * h : 256 + LANES * (h + 1)]
            core_out[t, h] = other.reshape(Z, PIECE, LANES).astype(BF16)
        core_copy(t).start()

        @pl.when(t == 1)
        def _():
            core_copy(0).wait_recv()
            for name in early:
                half, role, k = name
                value = block(0 if half == "a1" else 1, role, k)
                sum_out[R_SUM[name] - 4] = value.astype(BF16)
                piece_copy(name, x_next if half == "a1" else along_z(k)).start()

    for name in early:
        remember(name, x_next if name[0] == "a1" else along_z(name[2]))

    for name in in_order(sum_steps())[0]:
        if name[0] == "mul" or name in early:
            continue
        if name[0] == "a1":
            _, role, k = name
            value = block(0, role, k)
            if role == "plus":
                value = value + taken(("a1", "far", k))
            give(name, value, along_x(role))
        elif name[0] == "a2":
            k = name[1]
            value = block(0, "mine", k) + taken(("a1", "minus", k)) + taken(("a1", "plus", k))
            for earlier in (1, -1) if k == 0 else () if before(k) is None else (before(k),):
                value = value + taken(("a2", earlier))
            if k == 0:
                sum_a = value
            else:
                give(name, value, along_z(k))
        elif name[0] == "b1":
            _, role, k = name
            value = block(1, role, k)
            if before(k) is not None:
                value = value + taken(("b1", role, before(k)))
            give(name, value, along_z(k))
        else:
            role = name[1]
            value = block(1, role, 0) + taken(("b1", role, 1)) + taken(("b1", role, -1))
            for earlier in {"plus": ("far",), "mine": ("plus", "minus")}.get(role, ()):
                value = value + taken(("b2", earlier))
            if role == "mine":
                sum_b = value
            else:
                give(name, value, along_x(role))

    mine = 2 * y + c

    def spread(out, into, group, base, meanwhile=None):
        into[mine] = out[c]
        copies = []
        for n, (cc, yy) in enumerate(others):
            copies.append(
                send(out.at[cc], into.at[mine], at(x, z, cc, yy), group, base + n)
            )
        if meanwhile is not None:
            meanwhile()
        for copy in copies:
            copy.wait_recv()

    def read_table():
        def section_row(s, carry):
            def block_entry(b, carry):
                counts, kept = carry[:Y], carry[Y:]
                keeper = home[s, b]
                rank = jnp.int32(0)
                for n in range(Y):
                    rank = jnp.where(keeper == n, counts[n], rank)
                place = keeper * BLOCKS + rank
                position[s * BLOCKS + b] = place
                counts = tuple(counts[n] + jnp.where(keeper == n, 1, 0) for n in range(Y))
                here = place - y * BLOCKS
                kept = tuple(jnp.where(here == n, s * BLOCKS + b, kept[n]) for n in range(BLOCKS))
                return counts + kept

            return lax.fori_loop(0, BLOCKS, block_entry, carry)

        table = lax.fori_loop(0, Y, section_row, (jnp.int32(0),) * (Y + BLOCKS))
        for n in range(BLOCKS):
            order[n] = table[Y + n]

    for cc in range(2):
        rows = slice(HALF * cc, HALF * (cc + 1))
        g_out[cc] = jnp.concatenate([sum_a[rows], sum_b[rows]], axis=0).astype(BF16)
    spread(g_out, g_in, S_G, R_G, read_table)
    for s in range(Y):
        for cc in range(2):
            value = g_in[2 * s + cc].astype(F32)
            for jj in range(2):
                g_all[2 * cc + jj, BLOCKS * s : BLOCKS * (s + 1)] = value[HALF * jj : HALF * (jj + 1)].reshape(
                    BLOCKS, 8, LANES
                )

    for copy in state_copies:
        copy.wait()
    corr_one = 1.0 - 0.9**STEP
    corr_two = 1.0 - 0.99**STEP

    @pl.loop(0, BLOCKS)
    def _(i):
        f = order[i]
        s = lax.div(f, BLOCKS)
        b = f - s * BLOCKS
        limit = live_rows[s] - (dp * (4 * HALF) + b * 32)
        tile = lax.broadcasted_iota(jnp.int32, (8, LANES), 0)
        generator = tile * 0 + s < N_GEN
        for j in range(4):
            rows = pl.ds(i * 32 + j, 8, stride=4)
            grads = g_all[j, f]
            alive = tile * 4 + j < limit
            p, m1, m2, average = (state[n, rows, :] for n in range(4))
            first = jnp.where(alive, 0.9 * m1 + 0.1 * grads, m1)
            second = jnp.where(alive, 0.99 * m2 + 0.01 * grads * grads, m2)
            stepped = p - 0.0025 * (first / corr_one) / (jnp.sqrt(second / corr_two) + 1e-08)
            updated = jnp.where(alive, stepped, p)
            averaged = jnp.where(generator, 0.995 * average + 0.005 * updated, average)
            for n, value in enumerate((updated, first, second, averaged)):
                fresh[n, rows, :] = value
            h_all[j, pl.ds(pl.multiple_of(i * 8, 8), 8), :] = updated

    for cc in range(2):
        h_out[cc] = h_all[2 * cc : 2 * cc + 2].reshape(PIECE, LANES).astype(BF16)
    spread(h_out, h_in, S_H, R_H)
    fresh_copy = local(fresh, new_state, L_NEW)
    for s in range(Y):
        for cc in range(2):
            value = h_in[2 * s + cc].astype(F32)
            for jj in range(2):
                w_all[jj, cc, BLOCKS * s : BLOCKS * (s + 1)] = value[HALF * jj : HALF * (jj + 1)].reshape(
                    BLOCKS, 8, LANES
                )

    @pl.loop(0, BLOCKS)
    def _(b):
        place = position[y * BLOCKS + b]
        for cc in range(2):
            for jj in range(2):
                w_mine[jj, pl.ds(pl.multiple_of(HALF * cc + b * 8, 8), 8), :] = w_all[jj, cc, place]

    ja, jb = 2 * c, 2 * c + 1
    gathered[ja, x, z] = w_mine[0].astype(BF16)
    gathered[jb, x, z] = w_mine[1].astype(BF16)
    halves = {"wa": ja, "wb": jb}
    ways = {"z_next": z_next, "z_last": z_last, "x_next": x_next, "x_last": x_last}

    def go(name, way):
        _, i, k = name
        ref = gathered.at[halves[name[0]], xi(i), zi(k)]
        moving[name + (way,)] = send(ref, ref, ways[way], S_WAY, R_WAY[name + (way,)])

    def comes(name, axis, i):
        back = i + 1 if i < 0 else i - 1
        at_sender = (name[0], back, name[2]) if axis == "x" else (name[0], name[1], back)
        moving[at_sender + (axis + ("_next" if i < 0 else "_last"),)].wait_recv()

    seen, crossing, written = [], {}, []

    def write(j, xx, zz):
        lanes = pl.ds(pl.multiple_of(j * LANES, LANES), LANES)
        if xx is not None:
            source, target = gathered.at[j, xx], refreshed.at[xx, :, :, lanes]
        else:
            source, target = gathered.at[j, :, zz], refreshed.at[:, zz, :, lanes]
        written.append(local(source, target, L_OUT + len(written)))

    def cross(half, i, k):
        number = len(crossing)
        write(halves[half], None if half == "wb" else xi(i), zi(k))
        ref = gathered.at[halves[half], xi(i)] if half == "wa" else gathered.at[halves[half], :, zi(k)]
        crossing[half, i, k] = send(ref, ref, partner, S_ROW if half == "wa" else S_COLUMN, R_CROSS + number)

    for name in in_order(gather_steps())[0]:
        half, i, k = name
        first, second = (("z", k), ("x", i)) if half == "wa" else (("x", i), ("z", k))
        if second[1] != 0:
            comes(name, *second)
        elif first[1] != 0:
            comes(name, *first)
        for way in ways_on(name):
            go(name, way)
        seen.append(name)
        if half == "wa" and sum(n[:2] == name[:2] for n in seen) == Z:
            cross("wa", i, 0)
        if half == "wb" and sum(n[0] == "wb" and n[2] == k for n in seen) == X:
            cross("wb", 0, k)

    for (half, i, k), copy in crossing.items():
        copy.wait_recv()
        write(2 * (1 - c) + (half == "wb"), None if half == "wb" else xi(-i), zi(-k))
    for copy in written:
        copy.wait()
    fresh_copy.wait()

    for group, ref in (
        (S_CORE, core_out), (S_SUM, sum_out), (S_G, g_in.at[pl.ds(0, 7)]), (S_H, h_in.at[pl.ds(0, 7)]),
        (S_WAY, sum_out), (S_ROW, gathered.at[0]), (S_COLUMN, gathered.at[0]),
    ):
        pltpu.make_async_copy(ref, ref, send_sems.at[group]).wait()


def write_out(
    new_state, refreshed, new_params, new_moment1, new_moment2, new_ema, weights, state_buf, buf, in_sems, out_sems
):
    moves = [
        (new_state.at[n], state_buf.at[n], ref)
        for n, ref in enumerate((new_params, new_moment1, new_moment2, new_ema))
    ]
    for xx in range(X):
        for half in range(2):
            part = pl.ds(4 * half, 4)
            moves.append((refreshed.at[xx, part], buf.at[xx, part], weights.at[xx, part]))
    first = [pltpu.make_async_copy(a, b, in_sems.at[n]) for n, (a, b, _) in enumerate(moves)]
    second = [pltpu.make_async_copy(b, d, out_sems.at[n]) for n, (_, b, d) in enumerate(moves)]
    for copy in first:
        copy.start()
    for arrived, copy in zip(first, second):
        arrived.wait()
        copy.start()
    for copy in second:
        copy.wait()


def body(acts, grad_out, params, moment1, moment2, ema, live_rows, home):
    tokens = acts.shape[1]
    rows = (4 * HALF, LANES)
    any_space = pl.BlockSpec(memory_space=pl.ANY)
    smem = pl.BlockSpec(memory_space=pltpu.SMEM)
    plane = (Z, PIECE, LANES)
    chunk = (PIECE, LANES)
    outs = pl.pallas_call(
        kernel,
        out_shape=[
            jax.ShapeDtypeStruct((4,) + rows, F32),
            jax.ShapeDtypeStruct((X, Z, PIECE, 4 * LANES), BF16),
        ],
        in_specs=[any_space] * 6 + [smem] * 2,
        out_specs=[any_space] * 2,
        scratch_shapes=[
            pltpu.VMEM((X, tokens, Z * PIECE), BF16),
            pltpu.VMEM((tokens, 4 * LANES), BF16),
            pltpu.VMEM((X, 2) + plane, F32),
            pltpu.VMEM((X, 2) + plane, BF16),
            pltpu.VMEM((X, 2) + plane, BF16),
            pltpu.VMEM((N_SUM,) + chunk, BF16),
            pltpu.VMEM((N_SUM,) + chunk, BF16),
            pltpu.VMEM((2,) + chunk, BF16),
            pltpu.VMEM((2 * Y,) + chunk, BF16),
            pltpu.VMEM((4, Y * BLOCKS, 8, LANES), F32),
            pltpu.VMEM((4,) + rows, F32),
            pltpu.VMEM((4,) + rows, F32),
            pltpu.VMEM((4, HALF, LANES), F32),
            pltpu.VMEM((2,) + chunk, BF16),
            pltpu.VMEM((2 * Y,) + chunk, BF16),
            pltpu.VMEM((2, 2, Y * BLOCKS, 8, LANES), F32),
            pltpu.VMEM((2,) + chunk, F32),
            pltpu.VMEM((4, X) + plane, BF16),
            pltpu.SMEM((Y * BLOCKS,), jnp.int32),
            pltpu.SMEM((BLOCKS,), jnp.int32),
            pltpu.SemaphoreType.DMA((S_COLUMN + 1,)),
            pltpu.SemaphoreType.DMA((N_ARRIVE,)),
            pltpu.SemaphoreType.DMA((N_LOCAL,)),
        ],
        compiler_params=pltpu.CompilerParams(
            collective_id=0, has_side_effects=True, vmem_limit_bytes=56 * 2**20
        ),
    )(acts[0], grad_out[0], params[0], moment1[0], moment2[0], ema[0], live_rows, home)
    updated, first, second, averaged, weights = pl.pallas_call(
        write_out,
        out_shape=[jax.ShapeDtypeStruct(rows, F32)] * 4
        + [jax.ShapeDtypeStruct((X, Z, PIECE, 4 * LANES), BF16)],
        in_specs=[any_space] * 2,
        out_specs=[any_space] * 5,
        scratch_shapes=[
            pltpu.VMEM((4,) + rows, F32),
            pltpu.VMEM((X, Z, PIECE, 4 * LANES), BF16),
            pltpu.SemaphoreType.DMA((4 + 2 * X,)),
            pltpu.SemaphoreType.DMA((4 + 2 * X,)),
        ],
        compiler_params=pltpu.CompilerParams(vmem_limit_bytes=56 * 2**20),
    )(*outs)
    return (
        updated[None], first[None], second[None], averaged[None],
        weights.reshape(1, X * Z * PIECE, 4 * LANES),
    )


def solution(mesh):
    split = P("section", "dp", None)
    in_specs = (split,) * 6 + (P(), P())
    out_specs = (split,) * 4 + (P("section", None, None),)
    return jax.shard_map(body, mesh=mesh, in_specs=in_specs, out_specs=out_specs, check_vma=False)
```

```python
import jax
import jax.numpy as jnp
from jax import lax
from jax.experimental import pallas as pl
from jax.experimental.pallas import tpu as pltpu
from jax.sharding import PartitionSpec as P

N_GEN = 2
STEP = 100
MESH = pl.DeviceIdType.MESH
BF16, F32 = jnp.bfloat16, jnp.float32

X, Z, Y = 4, 8, 4
LANES = 128
HALF = 72
PIECE = 2 * HALF
BLOCKS = 9
OFFSETS = (2, 1, 3, 0)

LATENCY, PIECE_US, STEP_US = 2.2, 0.39, 0.12


def in_order(steps):
    left = {}

    def ahead(name):
        if name not in left:
            later = [
                ahead(other) + (LATENCY + PIECE_US if how == "sent" else 0.0)
                for other, (_, needs, _) in steps.items()
                for how, needed in needs
                if needed == name
            ]
            left[name] = steps[name][0] + max(later, default=0.0)
        return left[name]

    for name in steps:
        ahead(name)
    now, link_free, done, arrived, order = 0.0, {}, {}, {}, []
    while len(order) < len(steps):
        ready = []
        for name, (_, needs, _) in steps.items():
            if name in done:
                continue
            times = [(done if how == "done" else arrived).get(needed) for how, needed in needs]
            if None not in times:
                ready.append((max(times, default=0.0), -left[name], name))
        able = [(key, when, name) for when, key, name in ready if when <= now]
        if not able:
            now = min(ready)[0]
            continue
        name = min(able)[2]
        now += steps[name][0]
        done[name] = now
        for link, pieces in steps[name][2].items():
            link_free[link] = max(link_free.get(link, 0.0), now) + PIECE_US * pieces
            arrived[name] = max(arrived.get(name, 0.0), link_free[link] + LATENCY)
        order.append(name)
    return order, now


CHAIN = (4, 3, -3, 2, -2, 1, -1)
ROLES = ("far", "plus", "minus", "mine")


def before(k):
    return None if k in (4, -3) else k + 1 if k > 0 else k - 1


def sum_steps():
    steps = {}
    for t in range(X):
        steps["mul", t] = (1.4, [("done", ("mul", t - 1))] if t else [], {"core%d" % t: 0.5})

    def have(*blocks):
        return [("sent", ("mul", t)) for t in blocks]

    for k in CHAIN + (0,):
        steps["a1", "far", k] = (STEP_US, have(0), {"x": 1})
        steps["a1", "minus", k] = (STEP_US, have(1, 2), {"x": 1})
        steps["a1", "plus", k] = (STEP_US, have(1, 2) + [("sent", ("a1", "far", k))], {"x": 1})
        needs = have(3) + [("sent", ("a1", "plus", k)), ("sent", ("a1", "minus", k))]
        if k == 0:
            needs += [("sent", ("a2", 1)), ("sent", ("a2", -1))]
        elif before(k) is not None:
            needs.append(("sent", ("a2", before(k))))
        steps["a2", k] = (STEP_US, needs, {"z": 1} if k else {})
    for role in ROLES:
        block = {"far": (0,), "plus": (1, 2), "minus": (1, 2), "mine": (3,)}[role]
        for k in CHAIN:
            needs = have(*block)
            if before(k) is not None:
                needs.append(("sent", ("b1", role, before(k))))
            steps["b1", role, k] = (STEP_US, needs, {"z": 1})
        needs = have(*block) + [("sent", ("b1", role, 1)), ("sent", ("b1", role, -1))]
        needs += {
            "far": [], "minus": [], "plus": [("sent", ("b2", "far"))],
            "mine": [("sent", ("b2", "plus")), ("sent", ("b2", "minus"))],
        }[role]
        steps["b2", role] = (STEP_US, needs, {} if role == "mine" else {"x": 1})
    return steps


def gather_steps():
    steps = {}
    places = (0, -1, 1, -2, 2, -3, 3, -4)
    for k in places:
        links = {}
        for i in (0, -1, 1, -2):
            if i == 0:
                needs = [] if k == 0 else [("sent", ("wa", 0, k + 1 if k < 0 else k - 1))]
                links = {"z": (2 if k == 0 else 1 if k in (-1, -2, -3, 1, 2) else 0), "x": 2}
            else:
                needs = [("sent", ("wa", i + 1 if i < 0 else i - 1, k))]
                links = {"x": 1 if i == -1 else 0}
            steps["wa", i, k] = (STEP_US, needs, links)
            if k == 0:
                needs = [] if i == 0 else [("sent", ("wb", i + 1 if i < 0 else i - 1, 0))]
                links = {"x": (2 if i == 0 else 1 if i == -1 else 0), "z": 2}
            else:
                needs = [("sent", ("wb", i, k + 1 if k < 0 else k - 1))]
                links = {"z": 1 if k in (-1, -2, -3, 1, 2) else 0}
            steps["wb", i, k] = (STEP_US, needs, links)
    return steps


def numbered(names, start):
    return {name: start + n for n, name in enumerate(names)}


def onward(axis, i, size):
    if i == 0:
        return [axis + "_next", axis + "_last"]
    if i < 0:
        return [axis + "_next"] if i > -(size // 2) else []
    return [axis + "_last"] if i < size // 2 - 1 else []


def ways_on(name):
    half, i, k = name
    if half == "wa":
        return (onward("z", k, Z) if i == 0 else []) + onward("x", i, X)
    return (onward("x", i, X) if k == 0 else []) + onward("z", k, Z)


R_CORE = 0
R_SUM = numbered([name for name in sum_steps() if name[0] != "mul" and name not in (("a2", 0), ("b2", "mine"))], 4)
N_SUM = len(R_SUM)
R_G = 4 + N_SUM
R_STATE = R_G + 7
R_CROSS = R_STATE + 7
R_WAY = numbered([name + (way,) for name in gather_steps() for way in ways_on(name)], R_CROSS + 12)
N_ARRIVE = R_CROSS + 12 + len(R_WAY)
S_CORE, S_SUM, S_G, S_STATE, S_WAY, S_ROW, S_COLUMN = range(7)

L_ACTS = 0
L_COT = L_ACTS + 4
L_STATE = L_COT + 2
L_NEW = L_STATE + 4
L_OUT = L_NEW + 1
N_LOCAL = L_OUT + 1


def kernel(
    acts, cot, params, moment1, moment2, ema, live_rows, home, new_state, refreshed,
    acts_buf, cot_buf, own, core_out, core_in, sum_out, sum_in,
    g_out, g_in, g_all, g_mine, state, state_out, state_in, fresh, w_mine, gathered,
    position, order, send_sems, recv_sems, local_sems,
):
    dp = lax.axis_index("dp")
    y = lax.axis_index("section")
    c = lax.rem(dp, 2)
    z = lax.rem(lax.div(dp, 2), Z)
    x = lax.div(dp, 2 * Z)
    sign = 1 - 2 * c

    def xi(k):
        return lax.rem(x + sign * k + 2 * X, X)

    def zi(k):
        return lax.rem(z + sign * k + 2 * Z, Z)

    def at(xx, zz, cc, yy):
        return ((xx * Z + zz) * 2 + cc, yy)

    x_next, x_last = at(xi(1), z, c, y), at(xi(-1), z, c, y)
    z_next, z_last = at(x, zi(1), c, y), at(x, zi(-1), c, y)
    partner = at(x, z, 1 - c, y)
    others = []
    for dy in range(Y):
        for dc in range(2):
            if dy or dc:
                others.append((lax.rem(c + dc, 2), lax.rem(y + dy, Y)))

    barrier = pltpu.get_barrier_semaphore()
    greeted = [x_next, x_last, z_next, z_last] + [at(x, z, cc, yy) for cc, yy in others]
    for device in greeted:
        pl.semaphore_signal(barrier, inc=1, device_id=device, device_id_type=MESH)

    def local(src, dst, index):
        copy = pltpu.make_async_copy(src, dst, local_sems.at[index])
        copy.start()
        return copy

    def send(src, dst, device, group, number):
        copy = pltpu.make_async_remote_copy(
            src_ref=src, dst_ref=dst, send_sem=send_sems.at[group], recv_sem=recv_sems.at[number],
            device_id=device, device_id_type=MESH,
        )
        copy.start()
        return copy

    width = Z * PIECE
    state_copies = [
        local(ref, state.at[n], L_STATE + n) for n, ref in enumerate((params, moment1, moment2, ema))
    ]
    cot_copies = []
    for half in range(2):
        column = pl.multiple_of(256 * lax.rem(c + half, 2), 256)
        cot_copies.append(
            local(cot.at[:, pl.ds(column, 256)], cot_buf.at[:, pl.ds(256 * half, 256)], L_COT + half)
        )
    for t, offset in enumerate(OFFSETS):
        column = pl.multiple_of(width * lax.rem(x + offset, X), LANES)
        local(acts.at[:, pl.ds(column, width)], acts_buf.at[t], L_ACTS + t)
    for copy in state_copies[:3]:
        copy.wait()

    @pl.loop(0, BLOCKS)
    def _(i):
        for n in range(3):
            for j in range(4):
                state_out[j // 2, n, j % 2, i] = state[n, pl.ds(i * 32 + j, 8, stride=4), :]

    pl.semaphore_wait(barrier, len(greeted))

    for copy in cot_copies:
        copy.wait()

    mine = 2 * y + c

    def spread(out, into, group, base):
        into[mine] = out[c]
        return [
            send(out.at[cc], into.at[mine], at(x, z, cc, yy), group, base + n)
            for n, (cc, yy) in enumerate(others)
        ]

    state_moves = spread(state_out, state_in, S_STATE, R_STATE)

    def core_copy(t):
        return pltpu.make_async_remote_copy(
            src_ref=core_out.at[t], dst_ref=core_in.at[t],
            send_sem=send_sems.at[S_CORE], recv_sem=recv_sems.at[R_CORE + t],
            device_id=partner, device_id_type=MESH,
        )

    def read_table():
        def section_row(s, carry):
            def block_entry(b, carry):
                counts, kept = carry[:Y], carry[Y:]
                keeper = home[s, b]
                rank = jnp.int32(0)
                for n in range(Y):
                    rank = jnp.where(keeper == n, counts[n], rank)
                place = keeper * BLOCKS + rank
                position[s * BLOCKS + b] = place
                counts = tuple(counts[n] + jnp.where(keeper == n, 1, 0) for n in range(Y))
                here = place - y * BLOCKS
                kept = tuple(jnp.where(here == n, s * BLOCKS + b, kept[n]) for n in range(BLOCKS))
                return counts + kept

            return lax.fori_loop(0, BLOCKS, block_entry, carry)

        table = lax.fori_loop(0, Y, section_row, (jnp.int32(0),) * (Y + BLOCKS))
        for n in range(BLOCKS):
            order[n] = table[Y + n]

    here = {"far": 0, "plus": 1 + c, "minus": 2 - c, "mine": 3}
    needed = {"far": (0,), "plus": (1, 2), "minus": (1, 2), "mine": (3,)}
    crossed, moving = {0}, {}

    def block(h, role, k):
        for t in needed[role]:
            if t not in crossed:
                core_copy(t).wait_recv()
                crossed.add(t)
        return own[here[role], h, zi(k)] + core_in[here[role], h, zi(k)].astype(F32)

    def taken(name):
        moving[name].wait_recv()
        return sum_in[R_SUM[name] - 4].astype(F32)

    def piece_copy(name, device):
        slot = R_SUM[name] - 4
        return pltpu.make_async_remote_copy(
            src_ref=sum_out.at[slot], dst_ref=sum_in.at[slot],
            send_sem=send_sems.at[S_SUM], recv_sem=recv_sems.at[R_SUM[name]],
            device_id=device, device_id_type=MESH,
        )

    def remember(name, device):
        moving[name] = piece_copy(name, device)

    def give(name, value, device):
        sum_out[R_SUM[name] - 4] = value.astype(BF16)
        piece_copy(name, device).start()
        remember(name, device)

    def along_x(role):
        return x_last if role == "minus" else x_next

    def along_z(k):
        return z_next if k > 0 else z_last

    early = [("a1", "far", k) for k in CHAIN + (0,)] + [("b1", "far", 4), ("b1", "far", -3)]

    @pl.loop(0, X)
    def _(t):
        pltpu.make_async_copy(
            acts.at[:, pl.ds(0, width)], acts_buf.at[t], local_sems.at[L_ACTS + t]
        ).wait()
        product = lax.dot_general(
            acts_buf[t], cot_buf[...], (((0,), (0,)), ((), ())), preferred_element_type=F32
        )
        for h in range(2):
            own[t, h] = product[:, LANES * h : LANES * (h + 1)].reshape(Z, PIECE, LANES)
            other = product[:, 256 + LANES * h : 256 + LANES * (h + 1)]
            core_out[t, h] = other.reshape(Z, PIECE, LANES).astype(BF16)
        core_copy(t).start()

        @pl.when(t == 1)
        def _():
            core_copy(0).wait_recv()
            for name in early:
                half, role, k = name
                value = block(0 if half == "a1" else 1, role, k)
                sum_out[R_SUM[name] - 4] = value.astype(BF16)
                piece_copy(name, x_next if half == "a1" else along_z(k)).start()

    for name in early:
        remember(name, x_next if name[0] == "a1" else along_z(name[2]))

    for step, name in enumerate(in_order(sum_steps())[0]):
        if step == 40:
            read_table()
        if name[0] == "mul" or name in early:
            continue
        if name[0] == "a1":
            _, role, k = name
            value = block(0, role, k)
            if role == "plus":
                value = value + taken(("a1", "far", k))
            give(name, value, along_x(role))
        elif name[0] == "a2":
            k = name[1]
            value = block(0, "mine", k) + taken(("a1", "minus", k)) + taken(("a1", "plus", k))
            for earlier in (1, -1) if k == 0 else () if before(k) is None else (before(k),):
                value = value + taken(("a2", earlier))
            if k == 0:
                sum_a = value
            else:
                give(name, value, along_z(k))
        elif name[0] == "b1":
            _, role, k = name
            value = block(1, role, k)
            if before(k) is not None:
                value = value + taken(("b1", role, before(k)))
            give(name, value, along_z(k))
        else:
            role = name[1]
            value = block(1, role, 0) + taken(("b1", role, 1)) + taken(("b1", role, -1))
            for earlier in {"plus": ("far",), "mine": ("plus", "minus")}.get(role, ()):
                value = value + taken(("b2", earlier))
            if role == "mine":
                sum_b = value
            else:
                give(name, value, along_x(role))

    for cc in range(2):
        rows = slice(HALF * cc, HALF * (cc + 1))
        g_out[cc] = jnp.concatenate([sum_a[rows], sum_b[rows]], axis=0).astype(BF16)
    gradient_moves = spread(g_out, g_in, S_G, R_G)

    corr_one = 1.0 - 0.9**STEP
    corr_two = 1.0 - 0.99**STEP
    tile = lax.broadcasted_iota(jnp.int32, (8, LANES), 0)

    def adam(p, m1, m2, grads, alive):
        first = jnp.where(alive, 0.9 * m1 + 0.1 * grads, m1)
        second = jnp.where(alive, 0.99 * m2 + 0.01 * grads * grads, m2)
        stepped = p - 0.0025 * (first / corr_one) / (jnp.sqrt(second / corr_two) + 1e-08)
        return jnp.where(alive, stepped, p), first, second

    for jj, value in enumerate((sum_a, sum_b)):
        g_mine[jj] = value.astype(BF16).astype(F32).reshape(2, BLOCKS, 8, LANES)
    for copy in state_moves:
        copy.wait_recv()

    @pl.loop(0, BLOCKS)
    def _(b):
        place = position[y * BLOCKS + b]
        keeper = lax.div(place, BLOCKS)
        rank = place - keeper * BLOCKS
        for cc in range(2):
            limit = live_rows[y] - ((dp - c + cc) * (4 * HALF) + b * 32)
            for jj in range(2):
                alive = tile * 4 + (2 * c + jj) < limit
                p, m1, m2 = (state_in[2 * keeper + cc, n, jj, rank] for n in range(3))
                updated, _, _ = adam(p, m1, m2, g_mine[jj, cc, b], alive)
                w_mine[jj, pl.ds(pl.multiple_of(HALF * cc + b * 8, 8), 8), :] = updated

    def update_kept():
        for copy in gradient_moves:
            copy.wait_recv()
        state_copies[3].wait()
        for s in range(Y):
            for cc in range(2):
                value = g_in[2 * s + cc].astype(F32)
                for jj in range(2):
                    rows = value[HALF * jj : HALF * (jj + 1)]
                    g_all[2 * cc + jj, BLOCKS * s : BLOCKS * (s + 1)] = rows.reshape(BLOCKS, 8, LANES)

        @pl.loop(0, BLOCKS)
        def _(i):
            f = order[i]
            s = lax.div(f, BLOCKS)
            b = f - s * BLOCKS
            limit = live_rows[s] - (dp * (4 * HALF) + b * 32)
            generator = tile * 0 + s < N_GEN
            for j in range(4):
                rows = pl.ds(i * 32 + j, 8, stride=4)
                alive = tile * 4 + j < limit
                p, m1, m2, average = (state[n, rows, :] for n in range(4))
                updated, first, second = adam(p, m1, m2, g_all[j, f], alive)
                averaged = jnp.where(generator, 0.995 * average + 0.005 * updated, average)
                for n, value in enumerate((updated, first, second, averaged)):
                    fresh[n, rows, :] = value

        return local(fresh, new_state, L_NEW)

    ja, jb = 2 * c, 2 * c + 1
    gathered[ja, x, z] = w_mine[0].astype(BF16)
    gathered[jb, x, z] = w_mine[1].astype(BF16)
    halves = {"wa": ja, "wb": jb}
    ways = {"z_next": z_next, "z_last": z_last, "x_next": x_next, "x_last": x_last}

    def go(name, way):
        _, i, k = name
        ref = gathered.at[halves[name[0]], xi(i), zi(k)]
        moving[name + (way,)] = send(ref, ref, ways[way], S_WAY, R_WAY[name + (way,)])

    def comes(name, axis, i):
        back = i + 1 if i < 0 else i - 1
        at_sender = (name[0], back, name[2]) if axis == "x" else (name[0], name[1], back)
        moving[at_sender + (axis + ("_next" if i < 0 else "_last"),)].wait_recv()

    seen, crossing = [], {}

    def write(j, xx, zz):
        lanes = pl.ds(pl.multiple_of(j * LANES, LANES), LANES)
        if xx is not None:
            source, target = gathered.at[j, xx], refreshed.at[xx, :, :, lanes]
        else:
            source, target = gathered.at[j, :, zz], refreshed.at[:, zz, :, lanes]
        local(source, target, L_OUT)

    def cross(half, i, k):
        number = len(crossing)
        write(halves[half], None if half == "wb" else xi(i), zi(k))
        ref = gathered.at[halves[half], xi(i)] if half == "wa" else gathered.at[halves[half], :, zi(k)]
        crossing[half, i, k] = send(ref, ref, partner, S_ROW if half == "wa" else S_COLUMN, R_CROSS + number)

    for step, name in enumerate(in_order(gather_steps())[0]):
        if step == 44:
            fresh_copy = update_kept()
        half, i, k = name
        first, second = (("z", k), ("x", i)) if half == "wa" else (("x", i), ("z", k))
        if second[1] != 0:
            comes(name, *second)
        elif first[1] != 0:
            comes(name, *first)
        for way in ways_on(name):
            go(name, way)
        seen.append(name)
        if half == "wa" and sum(n[:2] == name[:2] for n in seen) == Z:
            cross("wa", i, 0)
        if half == "wb" and sum(n[0] == "wb" and n[2] == k for n in seen) == X:
            cross("wb", 0, k)

    for (half, i, k), copy in crossing.items():
        copy.wait_recv()
        write(2 * (1 - c) + (half == "wb"), None if half == "wb" else xi(-i), zi(-k))
    pltpu.make_async_copy(gathered, gathered, local_sems.at[L_OUT]).wait()
    fresh_copy.wait()

    for group, ref in (
        (S_CORE, core_out), (S_SUM, sum_out), (S_G, g_in.at[pl.ds(0, 7)]), (S_STATE, state_in.at[pl.ds(0, 7)]),
        (S_WAY, sum_out), (S_ROW, gathered.at[0]), (S_COLUMN, gathered.at[0]),
    ):
        pltpu.make_async_copy(ref, ref, send_sems.at[group]).wait()


def write_out(
    new_state, refreshed, new_params, new_moment1, new_moment2, new_ema, weights, state_buf, buf, in_sems, out_sems
):
    moves = [
        (new_state.at[n], state_buf.at[n], ref)
        for n, ref in enumerate((new_params, new_moment1, new_moment2, new_ema))
    ]
    for xx in range(X):
        for half in range(2):
            part = pl.ds(4 * half, 4)
            moves.append((refreshed.at[xx, part], buf.at[xx, part], weights.at[xx, part]))
    first = [pltpu.make_async_copy(a, b, in_sems.at[n]) for n, (a, b, _) in enumerate(moves)]
    second = [pltpu.make_async_copy(b, d, out_sems.at[n]) for n, (_, b, d) in enumerate(moves)]
    for copy in first:
        copy.start()
    for arrived, copy in zip(first, second):
        arrived.wait()
        copy.start()
    for copy in second:
        copy.wait()


def body(acts, grad_out, params, moment1, moment2, ema, live_rows, home):
    tokens = acts.shape[1]
    rows = (4 * HALF, LANES)
    any_space = pl.BlockSpec(memory_space=pl.ANY)
    smem = pl.BlockSpec(memory_space=pltpu.SMEM)
    plane = (Z, PIECE, LANES)
    chunk = (PIECE, LANES)
    outs = pl.pallas_call(
        kernel,
        out_shape=[
            jax.ShapeDtypeStruct((4,) + rows, F32),
            jax.ShapeDtypeStruct((X, Z, PIECE, 4 * LANES), BF16),
        ],
        in_specs=[any_space] * 6 + [smem] * 2,
        out_specs=[any_space] * 2,
        scratch_shapes=[
            pltpu.VMEM((X, tokens, Z * PIECE), BF16),
            pltpu.VMEM((tokens, 4 * LANES), BF16),
            pltpu.VMEM((X, 2) + plane, F32),
            pltpu.VMEM((X, 2) + plane, BF16),
            pltpu.VMEM((X, 2) + plane, BF16),
            pltpu.VMEM((N_SUM,) + chunk, BF16),
            pltpu.VMEM((N_SUM,) + chunk, BF16),
            pltpu.VMEM((2,) + chunk, BF16),
            pltpu.VMEM((2 * Y,) + chunk, BF16),
            pltpu.VMEM((4, Y * BLOCKS, 8, LANES), F32),
            pltpu.VMEM((2, 2, BLOCKS, 8, LANES), F32),
            pltpu.VMEM((4,) + rows, F32),
            pltpu.VMEM((2, 3, 2, BLOCKS, 8, LANES), F32),
            pltpu.VMEM((2 * Y, 3, 2, BLOCKS, 8, LANES), F32),
            pltpu.VMEM((4,) + rows, F32),
            pltpu.VMEM((2,) + chunk, F32),
            pltpu.VMEM((4, X) + plane, BF16),
            pltpu.SMEM((Y * BLOCKS,), jnp.int32),
            pltpu.SMEM((BLOCKS,), jnp.int32),
            pltpu.SemaphoreType.DMA((S_COLUMN + 1,)),
            pltpu.SemaphoreType.DMA((N_ARRIVE,)),
            pltpu.SemaphoreType.DMA((N_LOCAL,)),
        ],
        compiler_params=pltpu.CompilerParams(
            collective_id=0, has_side_effects=True, vmem_limit_bytes=56 * 2**20
        ),
    )(acts[0], grad_out[0], params[0], moment1[0], moment2[0], ema[0], live_rows, home)
    updated, first, second, averaged, weights = pl.pallas_call(
        write_out,
        out_shape=[jax.ShapeDtypeStruct(rows, F32)] * 4
        + [jax.ShapeDtypeStruct((X, Z, PIECE, 4 * LANES), BF16)],
        in_specs=[any_space] * 2,
        out_specs=[any_space] * 5,
        scratch_shapes=[
            pltpu.VMEM((4,) + rows, F32),
            pltpu.VMEM((X, Z, PIECE, 4 * LANES), BF16),
            pltpu.SemaphoreType.DMA((4 + 2 * X,)),
            pltpu.SemaphoreType.DMA((4 + 2 * X,)),
        ],
        compiler_params=pltpu.CompilerParams(vmem_limit_bytes=56 * 2**20),
    )(*outs)
    return (
        updated[None], first[None], second[None], averaged[None],
        weights.reshape(1, X * Z * PIECE, 4 * LANES),
    )


def solution(mesh):
    split = P("section", "dp", None)
    in_specs = (split,) * 6 + (P(), P())
    out_specs = (split,) * 4 + (P("section", None, None),)
    return jax.shard_map(body, mesh=mesh, in_specs=in_specs, out_specs=out_specs, check_vma=False)
```

```python
import jax
import jax.numpy as jnp
from jax import lax
from jax.experimental import pallas as pl
from jax.experimental.pallas import tpu as pltpu
from jax.sharding import PartitionSpec as P

N_GEN = 2
STEP = 100
MESH = pl.DeviceIdType.MESH
BF16, F32 = jnp.bfloat16, jnp.float32

X, Z, Y = 4, 8, 4
LANES = 128
HALF = 72
PIECE = 2 * HALF
BLOCKS = 9
OFFSETS = (2, 1, 3, 0)

LATENCY, PIECE_US, STEP_US = 2.2, 0.39, 0.12


def in_order(steps):
    left = {}

    def ahead(name):
        if name not in left:
            later = [
                ahead(other) + (LATENCY + PIECE_US if how == "sent" else 0.0)
                for other, (_, needs, _) in steps.items()
                for how, needed in needs
                if needed == name
            ]
            left[name] = steps[name][0] + max(later, default=0.0)
        return left[name]

    for name in steps:
        ahead(name)
    now, link_free, done, arrived, order = 0.0, {}, {}, {}, []
    while len(order) < len(steps):
        ready = []
        for name, (_, needs, _) in steps.items():
            if name in done:
                continue
            times = [(done if how == "done" else arrived).get(needed) for how, needed in needs]
            if None not in times:
                ready.append((max(times, default=0.0), -left[name], name))
        able = [(key, when, name) for when, key, name in ready if when <= now]
        if not able:
            now = min(ready)[0]
            continue
        name = min(able)[2]
        now += steps[name][0]
        done[name] = now
        for link, pieces in steps[name][2].items():
            link_free[link] = max(link_free.get(link, 0.0), now) + PIECE_US * pieces
            arrived[name] = max(arrived.get(name, 0.0), link_free[link] + LATENCY)
        order.append(name)
    return order, now


CHAIN = (4, 3, -3, 2, -2, 1, -1)
ROLES = ("far", "plus", "minus", "mine")


def before(k):
    return None if k in (4, -3) else k + 1 if k > 0 else k - 1


def sum_steps():
    steps = {}
    for t in range(X):
        steps["mul", t] = (1.4, [("done", ("mul", t - 1))] if t else [], {"core%d" % t: 0.5})

    def have(*blocks):
        return [("sent", ("mul", t)) for t in blocks]

    for k in CHAIN + (0,):
        steps["a1", "far", k] = (STEP_US, have(0), {"x": 1})
        steps["a1", "minus", k] = (STEP_US, have(1, 2), {"x": 1})
        steps["a1", "plus", k] = (STEP_US, have(1, 2) + [("sent", ("a1", "far", k))], {"x": 1})
        needs = have(3) + [("sent", ("a1", "plus", k)), ("sent", ("a1", "minus", k))]
        if k == 0:
            needs += [("sent", ("a2", 1)), ("sent", ("a2", -1))]
        elif before(k) is not None:
            needs.append(("sent", ("a2", before(k))))
        steps["a2", k] = (STEP_US, needs, {"z": 1} if k else {})
    for role in ROLES:
        block = {"far": (0,), "plus": (1, 2), "minus": (1, 2), "mine": (3,)}[role]
        for k in CHAIN:
            needs = have(*block)
            if before(k) is not None:
                needs.append(("sent", ("b1", role, before(k))))
            steps["b1", role, k] = (STEP_US, needs, {"z": 1})
        needs = have(*block) + [("sent", ("b1", role, 1)), ("sent", ("b1", role, -1))]
        needs += {
            "far": [], "minus": [], "plus": [("sent", ("b2", "far"))],
            "mine": [("sent", ("b2", "plus")), ("sent", ("b2", "minus"))],
        }[role]
        steps["b2", role] = (STEP_US, needs, {} if role == "mine" else {"x": 1})
    return steps


def gather_steps():
    steps = {}
    places = (0, -1, 1, -2, 2, -3, 3, -4)
    for k in places:
        links = {}
        for i in (0, -1, 1, -2):
            if i == 0:
                needs = [] if k == 0 else [("sent", ("wa", 0, k + 1 if k < 0 else k - 1))]
                links = {"z": (2 if k == 0 else 1 if k in (-1, -2, -3, 1, 2) else 0), "x": 2}
            else:
                needs = [("sent", ("wa", i + 1 if i < 0 else i - 1, k))]
                links = {"x": 1 if i == -1 else 0}
            steps["wa", i, k] = (STEP_US, needs, links)
            if k == 0:
                needs = [] if i == 0 else [("sent", ("wb", i + 1 if i < 0 else i - 1, 0))]
                links = {"x": (2 if i == 0 else 1 if i == -1 else 0), "z": 2}
            else:
                needs = [("sent", ("wb", i, k + 1 if k < 0 else k - 1))]
                links = {"z": 1 if k in (-1, -2, -3, 1, 2) else 0}
            steps["wb", i, k] = (STEP_US, needs, links)
    return steps


def numbered(names, start):
    return {name: start + n for n, name in enumerate(names)}


def onward(axis, i, size):
    if i == 0:
        return [axis + "_next", axis + "_last"]
    if i < 0:
        return [axis + "_next"] if i > -(size // 2) else []
    return [axis + "_last"] if i < size // 2 - 1 else []


def ways_on(name):
    half, i, k = name
    if half == "wa":
        return (onward("z", k, Z) if i == 0 else []) + onward("x", i, X)
    return (onward("x", i, X) if k == 0 else []) + onward("z", k, Z)


R_CORE = 0
R_SUM = numbered([name for name in sum_steps() if name[0] != "mul" and name not in (("a2", 0), ("b2", "mine"))], 4)
N_SUM = len(R_SUM)
R_G = 4 + N_SUM
R_STATE = R_G + 7
R_CROSS = R_STATE + 7
R_WAY = numbered([name + (way,) for name in gather_steps() for way in ways_on(name)], R_CROSS + 2 * Z)
N_ARRIVE = R_CROSS + 2 * Z + len(R_WAY)
S_CORE, S_SUM, S_G, S_STATE, S_WAY, S_CROSS = range(6)

L_ACTS = 0
L_COT = L_ACTS + 4
L_STATE = L_COT + 2
N_LOCAL = L_STATE + 4


def kernel(
    acts, cot, params, moment1, moment2, ema, live_rows, home, fresh, gathered,
    acts_buf, cot_buf, own, core_out, core_in, sum_out, sum_in,
    g_out, g_in, g_all, g_mine, state, state_out, state_in, w_mine,
    position, order, send_sems, recv_sems, local_sems,
):
    dp = lax.axis_index("dp")
    y = lax.axis_index("section")
    c = lax.rem(dp, 2)
    z = lax.rem(lax.div(dp, 2), Z)
    x = lax.div(dp, 2 * Z)
    sign = 1 - 2 * c

    def xi(k):
        return lax.rem(x + sign * k + 2 * X, X)

    def zi(k):
        return lax.rem(z + sign * k + 2 * Z, Z)

    def at(xx, zz, cc, yy):
        return ((xx * Z + zz) * 2 + cc, yy)

    x_next, x_last = at(xi(1), z, c, y), at(xi(-1), z, c, y)
    z_next, z_last = at(x, zi(1), c, y), at(x, zi(-1), c, y)
    partner = at(x, z, 1 - c, y)
    others = []
    for dy in range(Y):
        for dc in range(2):
            if dy or dc:
                others.append((lax.rem(c + dc, 2), lax.rem(y + dy, Y)))

    barrier = pltpu.get_barrier_semaphore()
    greeted = [x_next, x_last, z_next, z_last] + [at(x, z, cc, yy) for cc, yy in others]
    for device in greeted:
        pl.semaphore_signal(barrier, inc=1, device_id=device, device_id_type=MESH)

    def local(src, dst, index):
        copy = pltpu.make_async_copy(src, dst, local_sems.at[index])
        copy.start()
        return copy

    def send(src, dst, device, group, number):
        copy = pltpu.make_async_remote_copy(
            src_ref=src, dst_ref=dst, send_sem=send_sems.at[group], recv_sem=recv_sems.at[number],
            device_id=device, device_id_type=MESH,
        )
        copy.start()
        return copy

    width = Z * PIECE
    state_copies = [
        local(ref, state.at[n], L_STATE + n) for n, ref in enumerate((params, moment1, moment2, ema))
    ]
    cot_copies = []
    for half in range(2):
        column = pl.multiple_of(256 * lax.rem(c + half, 2), 256)
        cot_copies.append(
            local(cot.at[:, pl.ds(column, 256)], cot_buf.at[:, pl.ds(256 * half, 256)], L_COT + half)
        )
    for t, offset in enumerate(OFFSETS):
        column = pl.multiple_of(width * lax.rem(x + offset, X), LANES)
        local(acts.at[:, pl.ds(column, width)], acts_buf.at[t], L_ACTS + t)
    for copy in state_copies[:3]:
        copy.wait()

    @pl.loop(0, BLOCKS)
    def _(i):
        for n in range(3):
            for j in range(4):
                state_out[j // 2, n, j % 2, i] = state[n, pl.ds(i * 32 + j, 8, stride=4), :]

    pl.semaphore_wait(barrier, len(greeted))

    for copy in cot_copies:
        copy.wait()

    mine = 2 * y + c

    def spread(out, into, group, base):
        into[mine] = out[c]
        return [
            send(out.at[cc], into.at[mine], at(x, z, cc, yy), group, base + n)
            for n, (cc, yy) in enumerate(others)
        ]

    state_moves = spread(state_out, state_in, S_STATE, R_STATE)

    def core_copy(t):
        return pltpu.make_async_remote_copy(
            src_ref=core_out.at[t], dst_ref=core_in.at[t],
            send_sem=send_sems.at[S_CORE], recv_sem=recv_sems.at[R_CORE + t],
            device_id=partner, device_id_type=MESH,
        )

    def read_table():
        def section_row(s, carry):
            def block_entry(b, carry):
                counts, kept = carry[:Y], carry[Y:]
                keeper = home[s, b]
                rank = jnp.int32(0)
                for n in range(Y):
                    rank = jnp.where(keeper == n, counts[n], rank)
                place = keeper * BLOCKS + rank
                position[s * BLOCKS + b] = place
                counts = tuple(counts[n] + jnp.where(keeper == n, 1, 0) for n in range(Y))
                here = place - y * BLOCKS
                kept = tuple(jnp.where(here == n, s * BLOCKS + b, kept[n]) for n in range(BLOCKS))
                return counts + kept

            return lax.fori_loop(0, BLOCKS, block_entry, carry)

        table = lax.fori_loop(0, Y, section_row, (jnp.int32(0),) * (Y + BLOCKS))
        for n in range(BLOCKS):
            order[n] = table[Y + n]

    here = {"far": 0, "plus": 1 + c, "minus": 2 - c, "mine": 3}
    needed = {"far": (0,), "plus": (1, 2), "minus": (1, 2), "mine": (3,)}
    crossed, moving = {0}, {}

    def block(h, role, k):
        for t in needed[role]:
            if t not in crossed:
                core_copy(t).wait_recv()
                crossed.add(t)
        return own[here[role], h, zi(k)] + core_in[here[role], h, zi(k)].astype(F32)

    def taken(name):
        moving[name].wait_recv()
        return sum_in[R_SUM[name] - 4].astype(F32)

    def piece_copy(name, device):
        slot = R_SUM[name] - 4
        return pltpu.make_async_remote_copy(
            src_ref=sum_out.at[slot], dst_ref=sum_in.at[slot],
            send_sem=send_sems.at[S_SUM], recv_sem=recv_sems.at[R_SUM[name]],
            device_id=device, device_id_type=MESH,
        )

    def remember(name, device):
        moving[name] = piece_copy(name, device)

    def give(name, value, device):
        sum_out[R_SUM[name] - 4] = value.astype(BF16)
        piece_copy(name, device).start()
        remember(name, device)

    def along_x(role):
        return x_last if role == "minus" else x_next

    def along_z(k):
        return z_next if k > 0 else z_last

    early = [("a1", "far", k) for k in CHAIN + (0,)] + [("b1", "far", 4), ("b1", "far", -3)]

    @pl.loop(0, X)
    def _(t):
        pltpu.make_async_copy(
            acts.at[:, pl.ds(0, width)], acts_buf.at[t], local_sems.at[L_ACTS + t]
        ).wait()
        product = lax.dot_general(
            acts_buf[t], cot_buf[...], (((0,), (0,)), ((), ())), preferred_element_type=F32
        )
        for h in range(2):
            own[t, h] = product[:, LANES * h : LANES * (h + 1)].reshape(Z, PIECE, LANES)
            other = product[:, 256 + LANES * h : 256 + LANES * (h + 1)]
            core_out[t, h] = other.reshape(Z, PIECE, LANES).astype(BF16)
        core_copy(t).start()

        @pl.when(t == 1)
        def _():
            core_copy(0).wait_recv()
            for name in early:
                half, role, k = name
                value = block(0 if half == "a1" else 1, role, k)
                sum_out[R_SUM[name] - 4] = value.astype(BF16)
                piece_copy(name, x_next if half == "a1" else along_z(k)).start()

    for name in early:
        remember(name, x_next if name[0] == "a1" else along_z(name[2]))

    for step, name in enumerate(in_order(sum_steps())[0]):
        if step == 40:
            read_table()
        if name[0] == "mul" or name in early:
            continue
        if name[0] == "a1":
            _, role, k = name
            value = block(0, role, k)
            if role == "plus":
                value = value + taken(("a1", "far", k))
            give(name, value, along_x(role))
        elif name[0] == "a2":
            k = name[1]
            value = block(0, "mine", k) + taken(("a1", "minus", k)) + taken(("a1", "plus", k))
            for earlier in (1, -1) if k == 0 else () if before(k) is None else (before(k),):
                value = value + taken(("a2", earlier))
            if k == 0:
                sum_a = value
            else:
                give(name, value, along_z(k))
        elif name[0] == "b1":
            _, role, k = name
            value = block(1, role, k)
            if before(k) is not None:
                value = value + taken(("b1", role, before(k)))
            give(name, value, along_z(k))
        else:
            role = name[1]
            value = block(1, role, 0) + taken(("b1", role, 1)) + taken(("b1", role, -1))
            for earlier in {"plus": ("far",), "mine": ("plus", "minus")}.get(role, ()):
                value = value + taken(("b2", earlier))
            if role == "mine":
                sum_b = value
            else:
                give(name, value, along_x(role))

    for cc in range(2):
        rows = slice(HALF * cc, HALF * (cc + 1))
        g_out[cc] = jnp.concatenate([sum_a[rows], sum_b[rows]], axis=0).astype(BF16)
    gradient_moves = spread(g_out, g_in, S_G, R_G)

    corr_one = 1.0 - 0.9**STEP
    corr_two = 1.0 - 0.99**STEP
    tile = lax.broadcasted_iota(jnp.int32, (8, LANES), 0)

    def adam(p, m1, m2, grads, alive):
        first = jnp.where(alive, 0.9 * m1 + 0.1 * grads, m1)
        second = jnp.where(alive, 0.99 * m2 + 0.01 * grads * grads, m2)
        stepped = p - 0.0025 * (first / corr_one) / (jnp.sqrt(second / corr_two) + 1e-08)
        return jnp.where(alive, stepped, p), first, second

    for jj, value in enumerate((sum_a, sum_b)):
        g_mine[jj] = value.astype(BF16).astype(F32).reshape(2, BLOCKS, 8, LANES)
    for copy in state_moves:
        copy.wait_recv()

    @pl.loop(0, BLOCKS)
    def _(b):
        place = position[y * BLOCKS + b]
        keeper = lax.div(place, BLOCKS)
        rank = place - keeper * BLOCKS
        for cc in range(2):
            limit = live_rows[y] - ((dp - c + cc) * (4 * HALF) + b * 32)
            for jj in range(2):
                alive = tile * 4 + (2 * c + jj) < limit
                p, m1, m2 = (state_in[2 * keeper + cc, n, jj, rank] for n in range(3))
                updated, _, _ = adam(p, m1, m2, g_mine[jj, cc, b], alive)
                w_mine[jj, pl.ds(pl.multiple_of(HALF * cc + b * 8, 8), 8), :] = updated

    def update_kept():
        for copy in gradient_moves:
            copy.wait_recv()
        state_copies[3].wait()
        for s in range(Y):
            for cc in range(2):
                value = g_in[2 * s + cc].astype(F32)
                for jj in range(2):
                    rows = value[HALF * jj : HALF * (jj + 1)]
                    g_all[2 * cc + jj, BLOCKS * s : BLOCKS * (s + 1)] = rows.reshape(BLOCKS, 8, LANES)

        @pl.loop(0, BLOCKS)
        def _(i):
            f = order[i]
            s = lax.div(f, BLOCKS)
            b = f - s * BLOCKS
            limit = live_rows[s] - (dp * (4 * HALF) + b * 32)
            generator = tile * 0 + s < N_GEN
            for j in range(4):
                rows = pl.ds(i * 32 + j, 8, stride=4)
                alive = tile * 4 + j < limit
                p, m1, m2, average = (state[n, rows, :] for n in range(4))
                updated, first, second = adam(p, m1, m2, g_all[j, f], alive)
                averaged = jnp.where(generator, 0.995 * average + 0.005 * updated, average)
                for n, value in enumerate((updated, first, second, averaged)):
                    fresh[n, rows, :] = value

    ja, jb = 2 * c, 2 * c + 1
    gathered[ja, x, z] = w_mine[0].astype(BF16)
    gathered[jb, x, z] = w_mine[1].astype(BF16)
    halves = {"wa": ja, "wb": jb}
    ways = {"z_next": z_next, "z_last": z_last, "x_next": x_next, "x_last": x_last}

    def go(name, way):
        _, i, k = name
        ref = gathered.at[halves[name[0]], xi(i), zi(k)]
        moving[name + (way,)] = send(ref, ref, ways[way], S_WAY, R_WAY[name + (way,)])

    def comes(name, axis, i):
        back = i + 1 if i < 0 else i - 1
        at_sender = (name[0], back, name[2]) if axis == "x" else (name[0], name[1], back)
        moving[at_sender + (axis + ("_next" if i < 0 else "_last"),)].wait_recv()

    seen, crossing = [], {}

    def cross(half, k):
        ref = gathered.at[halves[half], :, zi(k)]
        crossing[half, k] = send(ref, ref, partner, S_CROSS, R_CROSS + len(crossing))

    def crossed_over(half, k):
        crossing[half, k].wait_recv()

    for step, name in enumerate(in_order(gather_steps())[0]):
        if step == 44:
            update_kept()
        half, i, k = name
        first, second = (("z", k), ("x", i)) if half == "wa" else (("x", i), ("z", k))
        if second[1] != 0:
            comes(name, *second)
        elif first[1] != 0:
            comes(name, *first)
        for way in ways_on(name):
            go(name, way)
        seen.append(name)
        if sum(n[0] == half and n[2] == k for n in seen) == X:
            cross(half, k)

    for column in crossing:
        crossed_over(*column)

    for group, ref in (
        (S_CORE, core_out), (S_SUM, sum_out), (S_G, g_in.at[pl.ds(0, 7)]), (S_STATE, state_in.at[pl.ds(0, 7)]),
        (S_WAY, sum_out), (S_CROSS, gathered.at[pl.ds(0, 2)]),
    ):
        pltpu.make_async_copy(ref, ref, send_sems.at[group]).wait()


def write_out(fresh, gathered, new_params, new_moment1, new_moment2, new_ema, weights, sems):
    moves = [
        (gathered.at[j, xx], weights.at[xx, :, :, pl.ds(LANES * j, LANES)]) for xx in range(X) for j in range(4)
    ]
    moves += [(fresh.at[n], ref) for n, ref in enumerate((new_params, new_moment1, new_moment2, new_ema))]
    copies = [pltpu.make_async_copy(source, target, sems.at[n]) for n, (source, target) in enumerate(moves)]
    for copy in copies:
        copy.start()
    for copy in copies:
        copy.wait()


def body(acts, grad_out, params, moment1, moment2, ema, live_rows, home):
    tokens = acts.shape[1]
    rows = (4 * HALF, LANES)
    any_space = pl.BlockSpec(memory_space=pl.ANY)
    smem = pl.BlockSpec(memory_space=pltpu.SMEM)
    plane = (Z, PIECE, LANES)
    chunk = (PIECE, LANES)
    outs = pl.pallas_call(
        kernel,
        out_shape=[
            pltpu.VMEM((4,) + rows, F32),
            pltpu.VMEM((4, X) + plane, BF16),
        ],
        in_specs=[any_space] * 6 + [smem] * 2,
        out_specs=[pl.BlockSpec(memory_space=pltpu.VMEM)] * 2,
        scratch_shapes=[
            pltpu.VMEM((X, tokens, Z * PIECE), BF16),
            pltpu.VMEM((tokens, 4 * LANES), BF16),
            pltpu.VMEM((X, 2) + plane, F32),
            pltpu.VMEM((X, 2) + plane, BF16),
            pltpu.VMEM((X, 2) + plane, BF16),
            pltpu.VMEM((N_SUM,) + chunk, BF16),
            pltpu.VMEM((N_SUM,) + chunk, BF16),
            pltpu.VMEM((2,) + chunk, BF16),
            pltpu.VMEM((2 * Y,) + chunk, BF16),
            pltpu.VMEM((4, Y * BLOCKS, 8, LANES), F32),
            pltpu.VMEM((2, 2, BLOCKS, 8, LANES), F32),
            pltpu.VMEM((4,) + rows, F32),
            pltpu.VMEM((2, 3, 2, BLOCKS, 8, LANES), F32),
            pltpu.VMEM((2 * Y, 3, 2, BLOCKS, 8, LANES), F32),
            pltpu.VMEM((2,) + chunk, F32),
            pltpu.SMEM((Y * BLOCKS,), jnp.int32),
            pltpu.SMEM((BLOCKS,), jnp.int32),
            pltpu.SemaphoreType.DMA((S_CROSS + 1,)),
            pltpu.SemaphoreType.DMA((N_ARRIVE,)),
            pltpu.SemaphoreType.DMA((N_LOCAL,)),
        ],
        compiler_params=pltpu.CompilerParams(
            collective_id=0, has_side_effects=True, vmem_limit_bytes=57 * 2**20
        ),
    )(acts[0], grad_out[0], params[0], moment1[0], moment2[0], ema[0], live_rows, home)
    updated, first, second, averaged, weights = pl.pallas_call(
        write_out,
        out_shape=[jax.ShapeDtypeStruct(rows, F32)] * 4
        + [jax.ShapeDtypeStruct((X, Z, PIECE, 4 * LANES), BF16)],
        in_specs=[pl.BlockSpec(memory_space=pltpu.VMEM)] * 2,
        out_specs=[any_space] * 5,
        scratch_shapes=[
            pltpu.SemaphoreType.DMA((4 * X + 4,)),
        ],
        compiler_params=pltpu.CompilerParams(vmem_limit_bytes=40 * 2**20),
    )(*outs)
    return (
        updated[None], first[None], second[None], averaged[None],
        weights.reshape(1, X * Z * PIECE, 4 * LANES),
    )


def solution(mesh):
    split = P("section", "dp", None)
    in_specs = (split,) * 6 + (P(), P())
    out_specs = (split,) * 4 + (P("section", None, None),)
    return jax.shard_map(body, mesh=mesh, in_specs=in_specs, out_specs=out_specs, check_vma=False)
```

```python
import jax
import jax.numpy as jnp
from jax import lax
from jax.experimental import pallas as pl
from jax.experimental.pallas import tpu as pltpu
from jax.sharding import PartitionSpec as P

N_GEN = 2
STEP = 100
MESH = pl.DeviceIdType.MESH
BF16, F32 = jnp.bfloat16, jnp.float32

X, Z, Y = 4, 8, 4
LANES = 128
HALF = 72
PIECE = 2 * HALF
BLOCKS = 9
OFFSETS = (2, 1, 3, 0)

LATENCY, PIECE_US, STEP_US = 1.7, 0.39, 0.4


def in_order(steps):
    left = {}

    def ahead(name):
        if name not in left:
            later = [
                ahead(other) + (LATENCY + PIECE_US if how == "sent" else 0.0)
                for other, (_, needs, _) in steps.items()
                for how, needed in needs
                if needed == name
            ]
            left[name] = steps[name][0] + max(later, default=0.0)
        return left[name]

    for name in steps:
        ahead(name)
    now, link_free, done, arrived, order = 0.0, {}, {}, {}, []
    while len(order) < len(steps):
        ready = []
        for name, (_, needs, _) in steps.items():
            if name in done:
                continue
            times = [(done if how == "done" else arrived).get(needed) for how, needed in needs]
            if None not in times:
                ready.append((max(times, default=0.0), -left[name], name))
        able = [(key, when, name) for when, key, name in ready if when <= now]
        if not able:
            now = min(ready)[0]
            continue
        name = min(able)[2]
        now += steps[name][0]
        done[name] = now
        for link, pieces in steps[name][2].items():
            link_free[link] = max(link_free.get(link, 0.0), now) + PIECE_US * pieces
            arrived[name] = max(arrived.get(name, 0.0), link_free[link] + LATENCY)
        order.append(name)
    return order, now


CHAIN = (4, 3, -3, 2, -2, 1, -1)
ROLES = ("far", "plus", "minus", "mine")


def before(k):
    return None if k in (4, -3) else k + 1 if k > 0 else k - 1


def sum_steps():
    steps = {}
    for t in range(X):
        steps["mul", t] = (1.4, [("done", ("mul", t - 1))] if t else [], {"core%d" % t: 0.5})

    def have(*blocks):
        return [("sent", ("mul", t)) for t in blocks]

    for k in CHAIN + (0,):
        steps["a1", "far", k] = (STEP_US, have(0), {"x": 1})
        steps["a1", "minus", k] = (STEP_US, have(1, 2), {"x": 1})
        steps["a1", "plus", k] = (STEP_US, have(1, 2) + [("sent", ("a1", "far", k))], {"x": 1})
        needs = have(3) + [("sent", ("a1", "plus", k)), ("sent", ("a1", "minus", k))]
        if k == 0:
            needs += [("sent", ("a2", 1)), ("sent", ("a2", -1))]
        elif before(k) is not None:
            needs.append(("sent", ("a2", before(k))))
        steps["a2", k] = (STEP_US, needs, {"z": 1} if k else {})
    for role in ROLES:
        block = {"far": (0,), "plus": (1, 2), "minus": (1, 2), "mine": (3,)}[role]
        for k in CHAIN:
            needs = have(*block)
            if before(k) is not None:
                needs.append(("sent", ("b1", role, before(k))))
            steps["b1", role, k] = (STEP_US, needs, {"z": 1})
        needs = have(*block) + [("sent", ("b1", role, 1)), ("sent", ("b1", role, -1))]
        needs += {
            "far": [], "minus": [], "plus": [("sent", ("b2", "far"))],
            "mine": [("sent", ("b2", "plus")), ("sent", ("b2", "minus"))],
        }[role]
        steps["b2", role] = (STEP_US, needs, {} if role == "mine" else {"x": 1})
    return steps


def gather_steps():
    steps = {}
    places = (0, -1, 1, -2, 2, -3, 3, -4)
    for k in places:
        links = {}
        for i in (0, -1, 1, -2):
            if i == 0:
                needs = [] if k == 0 else [("sent", ("wa", 0, k + 1 if k < 0 else k - 1))]
                links = {"z": (2 if k == 0 else 1 if k in (-1, -2, -3, 1, 2) else 0), "x": 2}
            else:
                needs = [("sent", ("wa", i + 1 if i < 0 else i - 1, k))]
                links = {"x": 1 if i == -1 else 0}
            steps["wa", i, k] = (STEP_US, needs, links)
            if k == 0:
                needs = [] if i == 0 else [("sent", ("wb", i + 1 if i < 0 else i - 1, 0))]
                links = {"x": (2 if i == 0 else 1 if i == -1 else 0), "z": 2}
            else:
                needs = [("sent", ("wb", i, k + 1 if k < 0 else k - 1))]
                links = {"z": 1 if k in (-1, -2, -3, 1, 2) else 0}
            steps["wb", i, k] = (STEP_US, needs, links)
    return steps


def numbered(names, start):
    return {name: start + n for n, name in enumerate(names)}


def onward(axis, i, size):
    if i == 0:
        return [axis + "_next", axis + "_last"]
    if i < 0:
        return [axis + "_next"] if i > -(size // 2) else []
    return [axis + "_last"] if i < size // 2 - 1 else []


def ways_on(name):
    half, i, k = name
    if half == "wa":
        return (onward("z", k, Z) if i == 0 else []) + onward("x", i, X)
    return (onward("x", i, X) if k == 0 else []) + onward("z", k, Z)


R_CORE = 0
R_SUM = numbered([name for name in sum_steps() if name[0] != "mul" and name not in (("a2", 0), ("b2", "mine"))], 4)
N_SUM = len(R_SUM)
R_G = 4 + N_SUM
R_STATE = R_G + 7
R_CROSS = R_STATE + 7
R_WAY = numbered([name + (way,) for name in gather_steps() for way in ways_on(name)], R_CROSS + 2 * Z)
N_ARRIVE = R_CROSS + 2 * Z + len(R_WAY)
S_CORE, S_SUM, S_G, S_STATE, S_WAY, S_CROSS = range(6)

L_ACTS = 0
L_COT = L_ACTS + 4
L_STATE = L_COT + 2
N_LOCAL = L_STATE + 4


def kernel(
    acts, cot, params, moment1, moment2, ema, live_rows, home, fresh, gathered,
    acts_buf, cot_buf, own, core_out, core_in, sum_out, sum_in,
    g_out, g_in, g_all, state, state_out, state_in, state_mine,
    position, order, send_sems, recv_sems, local_sems,
):
    dp = lax.axis_index("dp")
    y = lax.axis_index("section")
    c = lax.rem(dp, 2)
    z = lax.rem(lax.div(dp, 2), Z)
    x = lax.div(dp, 2 * Z)
    sign = 1 - 2 * c

    def xi(k):
        return lax.rem(x + sign * k + 2 * X, X)

    def zi(k):
        return lax.rem(z + sign * k + 2 * Z, Z)

    def at(xx, zz, cc, yy):
        return ((xx * Z + zz) * 2 + cc, yy)

    x_next, x_last = at(xi(1), z, c, y), at(xi(-1), z, c, y)
    z_next, z_last = at(x, zi(1), c, y), at(x, zi(-1), c, y)
    partner = at(x, z, 1 - c, y)
    others = []
    for dy in range(Y):
        for dc in range(2):
            if dy or dc:
                others.append((lax.rem(c + dc, 2), lax.rem(y + dy, Y)))

    barrier = pltpu.get_barrier_semaphore()
    greeted = [x_next, x_last, z_next, z_last] + [at(x, z, cc, yy) for cc, yy in others]
    for device in greeted:
        pl.semaphore_signal(barrier, inc=1, device_id=device, device_id_type=MESH)

    def local(src, dst, index):
        copy = pltpu.make_async_copy(src, dst, local_sems.at[index])
        copy.start()
        return copy

    def send(src, dst, device, group, number):
        copy = pltpu.make_async_remote_copy(
            src_ref=src, dst_ref=dst, send_sem=send_sems.at[group], recv_sem=recv_sems.at[number],
            device_id=device, device_id_type=MESH,
        )
        copy.start()
        return copy

    width = Z * PIECE
    cot_copies = []
    for half in range(2):
        column = pl.multiple_of(256 * lax.rem(c + half, 2), 256)
        cot_copies.append(
            local(cot.at[:, pl.ds(column, 256)], cot_buf.at[:, pl.ds(256 * half, 256)], L_COT + half)
        )

    def load_acts(t, offset):
        column = pl.multiple_of(width * lax.rem(x + offset, X), LANES)
        local(acts.at[:, pl.ds(column, width)], acts_buf.at[t], L_ACTS + t)

    load_acts(0, OFFSETS[0])
    state_copies = [
        local(ref, state.at[n], L_STATE + n) for n, ref in enumerate((params, moment1, moment2, ema))
    ]
    load_acts(1, OFFSETS[1])

    for copy in state_copies[:3]:
        copy.wait()

    @pl.loop(0, BLOCKS)
    def _(i):
        for n in range(3):
            for j in range(4):
                state_out[j // 2, n, j % 2, i] = state[n, pl.ds(i * 32 + j, 8, stride=4), :]

    pl.semaphore_wait(barrier, len(greeted))

    for copy in cot_copies:
        copy.wait()

    mine = 2 * y + c

    def spread(out, into, group, base):
        into[mine] = out[c]
        return [
            send(out.at[cc], into.at[mine], at(x, z, cc, yy), group, base + n)
            for n, (cc, yy) in enumerate(others)
        ]

    state_moves = spread(state_out, state_in, S_STATE, R_STATE)

    def core_copy(t):
        return pltpu.make_async_remote_copy(
            src_ref=core_out.at[t], dst_ref=core_in.at[t],
            send_sem=send_sems.at[S_CORE], recv_sem=recv_sems.at[R_CORE + t],
            device_id=partner, device_id_type=MESH,
        )

    def read_table():
        def section_row(s, carry):
            def block_entry(b, carry):
                counts, kept = carry[:Y], carry[Y:]
                keeper = home[s, b]
                rank = jnp.int32(0)
                for n in range(Y):
                    rank = jnp.where(keeper == n, counts[n], rank)
                place = keeper * BLOCKS + rank
                position[s * BLOCKS + b] = place
                counts = tuple(counts[n] + jnp.where(keeper == n, 1, 0) for n in range(Y))
                here = place - y * BLOCKS
                kept = tuple(jnp.where(here == n, s * BLOCKS + b, kept[n]) for n in range(BLOCKS))
                return counts + kept

            return lax.fori_loop(0, BLOCKS, block_entry, carry)

        table = lax.fori_loop(0, Y, section_row, (jnp.int32(0),) * (Y + BLOCKS))
        for n in range(BLOCKS):
            order[n] = table[Y + n]

    here = {"far": 0, "plus": 1 + c, "minus": 2 - c, "mine": 3}
    needed = {"far": (0,), "plus": (1, 2), "minus": (1, 2), "mine": (3,)}
    crossed, moving = {0}, {}

    def block(h, role, k):
        for t in needed[role]:
            if t not in crossed:
                core_copy(t).wait_recv()
                crossed.add(t)
        return own[here[role], h, zi(k)] + core_in[here[role], h, zi(k)].astype(F32)

    def taken(name):
        moving[name].wait_recv()
        return sum_in[R_SUM[name] - 4].astype(F32)

    def piece_copy(name, device):
        slot = R_SUM[name] - 4
        return pltpu.make_async_remote_copy(
            src_ref=sum_out.at[slot], dst_ref=sum_in.at[slot],
            send_sem=send_sems.at[S_SUM], recv_sem=recv_sems.at[R_SUM[name]],
            device_id=device, device_id_type=MESH,
        )

    def remember(name, device):
        moving[name] = piece_copy(name, device)

    def give(name, value, device):
        sum_out[R_SUM[name] - 4] = value.astype(BF16)
        piece_copy(name, device).start()
        remember(name, device)

    def along_x(role):
        return x_last if role == "minus" else x_next

    def along_z(k):
        return z_next if k > 0 else z_last

    early = [("a1", "far", k) for k in CHAIN + (0,)] + [("b1", "far", 4), ("b1", "far", -3)]

    @pl.loop(0, X)
    def _(t):
        pltpu.make_async_copy(
            acts.at[:, pl.ds(0, width)], acts_buf.at[t], local_sems.at[L_ACTS + t]
        ).wait()

        @pl.when(t < X - 2)
        def _():
            load_acts(t + 2, lax.select(t == 0, OFFSETS[2], OFFSETS[3]))

        product = lax.dot_general(
            acts_buf[t], cot_buf[...], (((0,), (0,)), ((), ())), preferred_element_type=F32
        )
        for h in range(2):
            own[t, h] = product[:, LANES * h : LANES * (h + 1)].reshape(Z, PIECE, LANES)
            other = product[:, 256 + LANES * h : 256 + LANES * (h + 1)]
            core_out[t, h] = other.reshape(Z, PIECE, LANES).astype(BF16)
        core_copy(t).start()

        @pl.when(t == 1)
        def _():
            core_copy(0).wait_recv()
            for name in early:
                half, role, k = name
                value = block(0 if half == "a1" else 1, role, k)
                sum_out[R_SUM[name] - 4] = value.astype(BF16)
                piece_copy(name, x_next if half == "a1" else along_z(k)).start()

    for name in early:
        remember(name, x_next if name[0] == "a1" else along_z(name[2]))

    def collect():
        for copy in state_moves:
            copy.wait_recv()

        @pl.loop(0, BLOCKS)
        def _(b):
            place = position[y * BLOCKS + b]
            keeper = lax.div(place, BLOCKS)
            rank = place - keeper * BLOCKS
            for cc in range(2):
                for n in range(3):
                    for jj in range(2):
                        state_mine[n, jj, cc, b] = state_in[2 * keeper + cc, n, jj, rank]

    for step, name in enumerate(in_order(sum_steps())[0]):
        if step == 40:
            read_table()
        if step == len(sum_steps()) - 3:
            collect()
        if name[0] == "mul" or name in early:
            continue
        if name[0] == "a1":
            _, role, k = name
            value = block(0, role, k)
            if role == "plus":
                value = value + taken(("a1", "far", k))
            give(name, value, along_x(role))
        elif name[0] == "a2":
            k = name[1]
            value = block(0, "mine", k) + taken(("a1", "minus", k)) + taken(("a1", "plus", k))
            for earlier in (1, -1) if k == 0 else () if before(k) is None else (before(k),):
                value = value + taken(("a2", earlier))
            if k == 0:
                sum_a = value
            else:
                give(name, value, along_z(k))
        elif name[0] == "b1":
            _, role, k = name
            value = block(1, role, k)
            if before(k) is not None:
                value = value + taken(("b1", role, before(k)))
            give(name, value, along_z(k))
        else:
            role = name[1]
            value = block(1, role, 0) + taken(("b1", role, 1)) + taken(("b1", role, -1))
            for earlier in {"plus": ("far",), "mine": ("plus", "minus")}.get(role, ()):
                value = value + taken(("b2", earlier))
            if role == "mine":
                sum_b = value
            else:
                give(name, value, along_x(role))

    corr_one = 1.0 - 0.9**STEP
    corr_two = 1.0 - 0.99**STEP
    tile = lax.broadcasted_iota(jnp.int32, (8, LANES), 0)

    def adam(p, m1, m2, grads, alive):
        first = jnp.where(alive, 0.9 * m1 + 0.1 * grads, m1)
        second = jnp.where(alive, 0.99 * m2 + 0.01 * grads * grads, m2)
        stepped = p - 0.0025 * (first / corr_one) / (jnp.sqrt(second / corr_two) + 1e-08)
        return jnp.where(alive, stepped, p), first, second

    sums = [value.astype(BF16).astype(F32) for value in (sum_a, sum_b)]
    limit = live_rows[y] - (dp - c) * (4 * HALF)
    row = lax.broadcasted_iota(jnp.int32, (PIECE, LANES), 0) * 4
    for jj in range(2):
        p, m1, m2 = (state_mine[n, jj].reshape(PIECE, LANES) for n in range(3))
        updated, _, _ = adam(p, m1, m2, sums[jj], row + (2 * c + jj) < limit)
        gathered[2 * c + jj, x, z] = updated.astype(BF16)

    def send_gradient():
        for cc in range(2):
            rows = slice(HALF * cc, HALF * (cc + 1))
            g_out[cc] = jnp.concatenate([value[rows] for value in sums], axis=0).astype(BF16)
        return spread(g_out, g_in, S_G, R_G)

    def update_kept(gradient_moves):
        for copy in gradient_moves:
            copy.wait_recv()
        state_copies[3].wait()
        for s in range(Y):
            for cc in range(2):
                value = g_in[2 * s + cc].astype(F32)
                for jj in range(2):
                    rows = value[HALF * jj : HALF * (jj + 1)]
                    g_all[2 * cc + jj, BLOCKS * s : BLOCKS * (s + 1)] = rows.reshape(BLOCKS, 8, LANES)

        @pl.loop(0, BLOCKS)
        def _(i):
            f = order[i]
            s = lax.div(f, BLOCKS)
            b = f - s * BLOCKS
            limit = live_rows[s] - (dp * (4 * HALF) + b * 32)
            generator = tile * 0 + s < N_GEN
            for j in range(4):
                rows = pl.ds(i * 32 + j, 8, stride=4)
                alive = tile * 4 + j < limit
                p, m1, m2, average = (state[n, rows, :] for n in range(4))
                updated, first, second = adam(p, m1, m2, g_all[j, f], alive)
                averaged = jnp.where(generator, 0.995 * average + 0.005 * updated, average)
                for n, value in enumerate((updated, first, second, averaged)):
                    fresh[n, rows, :] = value

    ja, jb = 2 * c, 2 * c + 1
    halves = {"wa": ja, "wb": jb}
    ways = {"z_next": z_next, "z_last": z_last, "x_next": x_next, "x_last": x_last}

    def go(name, way):
        _, i, k = name
        ref = gathered.at[halves[name[0]], xi(i), zi(k)]
        moving[name + (way,)] = send(ref, ref, ways[way], S_WAY, R_WAY[name + (way,)])

    def comes(name, axis, i):
        back = i + 1 if i < 0 else i - 1
        at_sender = (name[0], back, name[2]) if axis == "x" else (name[0], name[1], back)
        moving[at_sender + (axis + ("_next" if i < 0 else "_last"),)].wait_recv()

    seen, crossing = [], {}

    def cross(half, k):
        ref = gathered.at[halves[half], :, zi(k)]
        crossing[half, k] = send(ref, ref, partner, S_CROSS, R_CROSS + len(crossing))

    def crossed_over(half, k):
        crossing[half, k].wait_recv()

    gather_order = in_order(gather_steps())[0]
    last_sent = max(step for step, name in enumerate(gather_order) if ways_on(name))
    for step, name in enumerate(gather_order):
        if step == 6:
            gradient_moves = send_gradient()
        if step == last_sent + 1:
            update_kept(gradient_moves)
        half, i, k = name
        first, second = (("z", k), ("x", i)) if half == "wa" else (("x", i), ("z", k))
        if second[1] != 0:
            comes(name, *second)
        elif first[1] != 0:
            comes(name, *first)
        for way in ways_on(name):
            go(name, way)
        seen.append(name)
        if sum(n[0] == half and n[2] == k for n in seen) == X:
            cross(half, k)

    for column in crossing:
        crossed_over(*column)

    for group, ref in (
        (S_CORE, core_out), (S_SUM, sum_out), (S_G, g_in.at[pl.ds(0, 7)]), (S_STATE, state_in.at[pl.ds(0, 7)]),
        (S_WAY, sum_out), (S_CROSS, gathered.at[pl.ds(0, 2)]),
    ):
        pltpu.make_async_copy(ref, ref, send_sems.at[group]).wait()


def write_out(fresh, gathered, new_params, new_moment1, new_moment2, new_ema, weights, sems):
    moves = [
        (gathered.at[j, xx], weights.at[xx, :, :, pl.ds(LANES * j, LANES)]) for xx in range(X) for j in range(4)
    ]
    moves += [(fresh.at[n], ref) for n, ref in enumerate((new_params, new_moment1, new_moment2, new_ema))]
    copies = [pltpu.make_async_copy(source, target, sems.at[n]) for n, (source, target) in enumerate(moves)]
    for copy in copies:
        copy.start()
    for copy in copies:
        copy.wait()


def body(acts, grad_out, params, moment1, moment2, ema, live_rows, home):
    tokens = acts.shape[1]
    rows = (4 * HALF, LANES)
    any_space = pl.BlockSpec(memory_space=pl.ANY)
    smem = pl.BlockSpec(memory_space=pltpu.SMEM)
    plane = (Z, PIECE, LANES)
    chunk = (PIECE, LANES)
    outs = pl.pallas_call(
        kernel,
        out_shape=[
            pltpu.VMEM((4,) + rows, F32),
            pltpu.VMEM((4, X) + plane, BF16),
        ],
        in_specs=[any_space] * 6 + [smem] * 2,
        out_specs=[pl.BlockSpec(memory_space=pltpu.VMEM)] * 2,
        scratch_shapes=[
            pltpu.VMEM((X, tokens, Z * PIECE), BF16),
            pltpu.VMEM((tokens, 4 * LANES), BF16),
            pltpu.VMEM((X, 2) + plane, F32),
            pltpu.VMEM((X, 2) + plane, BF16),
            pltpu.VMEM((X, 2) + plane, BF16),
            pltpu.VMEM((N_SUM,) + chunk, BF16),
            pltpu.VMEM((N_SUM,) + chunk, BF16),
            pltpu.VMEM((2,) + chunk, BF16),
            pltpu.VMEM((2 * Y,) + chunk, BF16),
            pltpu.VMEM((4, Y * BLOCKS, 8, LANES), F32),
            pltpu.VMEM((4,) + rows, F32),
            pltpu.VMEM((2, 3, 2, BLOCKS, 8, LANES), F32),
            pltpu.VMEM((2 * Y, 3, 2, BLOCKS, 8, LANES), F32),
            pltpu.VMEM((3, 2, 2, BLOCKS, 8, LANES), F32),
            pltpu.SMEM((Y * BLOCKS,), jnp.int32),
            pltpu.SMEM((BLOCKS,), jnp.int32),
            pltpu.SemaphoreType.DMA((S_CROSS + 1,)),
            pltpu.SemaphoreType.DMA((N_ARRIVE,)),
            pltpu.SemaphoreType.DMA((N_LOCAL,)),
        ],
        compiler_params=pltpu.CompilerParams(
            collective_id=0, has_side_effects=True, vmem_limit_bytes=57 * 2**20
        ),
    )(acts[0], grad_out[0], params[0], moment1[0], moment2[0], ema[0], live_rows, home)
    updated, first, second, averaged, weights = pl.pallas_call(
        write_out,
        out_shape=[jax.ShapeDtypeStruct(rows, F32)] * 4
        + [jax.ShapeDtypeStruct((X, Z, PIECE, 4 * LANES), BF16)],
        in_specs=[pl.BlockSpec(memory_space=pltpu.VMEM)] * 2,
        out_specs=[any_space] * 5,
        scratch_shapes=[
            pltpu.SemaphoreType.DMA((4 * X + 4,)),
        ],
        compiler_params=pltpu.CompilerParams(vmem_limit_bytes=40 * 2**20),
    )(*outs)
    return (
        updated[None], first[None], second[None], averaged[None],
        weights.reshape(1, X * Z * PIECE, 4 * LANES),
    )


def solution(mesh):
    split = P("section", "dp", None)
    in_specs = (split,) * 6 + (P(), P())
    out_specs = (split,) * 4 + (P("section", None, None),)
    return jax.shard_map(body, mesh=mesh, in_specs=in_specs, out_specs=out_specs, check_vma=False)
```

```python
import jax
import jax.numpy as jnp
from jax import lax
from jax.experimental import pallas as pl
from jax.experimental.pallas import tpu as pltpu
from jax.sharding import PartitionSpec as P

N_GEN = 2
STEP = 100
MESH = pl.DeviceIdType.MESH
BF16, F32 = jnp.bfloat16, jnp.float32

X, Z, Y = 4, 8, 4
LANES = 128
HALF = 72
PIECE = 2 * HALF
BLOCKS = 9
OFFSETS = (2, 1, 3, 0)

LATENCY, PIECE_US, STEP_US = 1.7, 0.39, 0.4


def in_order(steps):
    left = {}

    def ahead(name):
        if name not in left:
            later = [
                ahead(other) + (LATENCY + PIECE_US if how == "sent" else 0.0)
                for other, (_, needs, _) in steps.items()
                for how, needed in needs
                if needed == name
            ]
            left[name] = steps[name][0] + max(later, default=0.0)
        return left[name]

    for name in steps:
        ahead(name)
    now, link_free, done, arrived, order = 0.0, {}, {}, {}, []
    while len(order) < len(steps):
        ready = []
        for name, (_, needs, _) in steps.items():
            if name in done:
                continue
            times = [(done if how == "done" else arrived).get(needed) for how, needed in needs]
            if None not in times:
                ready.append((max(times, default=0.0), -left[name], name))
        able = [(key, when, name) for when, key, name in ready if when <= now]
        if not able:
            now = min(ready)[0]
            continue
        name = min(able)[2]
        now += steps[name][0]
        done[name] = now
        for link, pieces in steps[name][2].items():
            link_free[link] = max(link_free.get(link, 0.0), now) + PIECE_US * pieces
            arrived[name] = max(arrived.get(name, 0.0), link_free[link] + LATENCY)
        order.append(name)
    return order, now


CHAIN = (4, 3, -3, 2, -2, 1, -1)
ROLES = ("far", "plus", "minus", "mine")


def before(k):
    return None if k in (4, -3) else k + 1 if k > 0 else k - 1


def sum_steps():
    steps = {}
    for t in range(X):
        steps["mul", t] = (1.4, [("done", ("mul", t - 1))] if t else [], {"core%d" % t: 0.5})

    def have(*blocks):
        return [("sent", ("mul", t)) for t in blocks]

    for k in CHAIN + (0,):
        steps["a1", "far", k] = (STEP_US, have(0), {"x": 1})
        steps["a1", "minus", k] = (STEP_US, have(1, 2), {"x": 1})
        steps["a1", "plus", k] = (STEP_US, have(1, 2) + [("sent", ("a1", "far", k))], {"x": 1})
        needs = have(3) + [("sent", ("a1", "plus", k)), ("sent", ("a1", "minus", k))]
        if k == 0:
            needs += [("sent", ("a2", 1)), ("sent", ("a2", -1))]
        elif before(k) is not None:
            needs.append(("sent", ("a2", before(k))))
        steps["a2", k] = (STEP_US, needs, {"z": 1} if k else {})
    for role in ROLES:
        block = {"far": (0,), "plus": (1, 2), "minus": (1, 2), "mine": (3,)}[role]
        for k in CHAIN:
            needs = have(*block)
            if before(k) is not None:
                needs.append(("sent", ("b1", role, before(k))))
            steps["b1", role, k] = (STEP_US, needs, {"z": 1})
        needs = have(*block) + [("sent", ("b1", role, 1)), ("sent", ("b1", role, -1))]
        needs += {
            "far": [], "minus": [], "plus": [("sent", ("b2", "far"))],
            "mine": [("sent", ("b2", "plus")), ("sent", ("b2", "minus"))],
        }[role]
        steps["b2", role] = (STEP_US, needs, {} if role == "mine" else {"x": 1})
    return steps


def gather_steps():
    steps = {}
    places = (0, -1, 1, -2, 2, -3, 3, -4)
    for k in places:
        links = {}
        for i in (0, -1, 1, -2):
            if i == 0:
                needs = [] if k == 0 else [("sent", ("wa", 0, k + 1 if k < 0 else k - 1))]
                links = {"z": (2 if k == 0 else 1 if k in (-1, -2, -3, 1, 2) else 0), "x": 2}
            else:
                needs = [("sent", ("wa", i + 1 if i < 0 else i - 1, k))]
                links = {"x": 1 if i == -1 else 0}
            steps["wa", i, k] = (STEP_US, needs, links)
            if k == 0:
                needs = [] if i == 0 else [("sent", ("wb", i + 1 if i < 0 else i - 1, 0))]
                links = {"x": (2 if i == 0 else 1 if i == -1 else 0), "z": 2}
            else:
                needs = [("sent", ("wb", i, k + 1 if k < 0 else k - 1))]
                links = {"z": 1 if k in (-1, -2, -3, 1, 2) else 0}
            steps["wb", i, k] = (STEP_US, needs, links)
    return steps


def numbered(names, start):
    return {name: start + n for n, name in enumerate(names)}


def onward(axis, i, size):
    if i == 0:
        return [axis + "_next", axis + "_last"]
    if i < 0:
        return [axis + "_next"] if i > -(size // 2) else []
    return [axis + "_last"] if i < size // 2 - 1 else []


def ways_on(name):
    half, i, k = name
    if half == "wa":
        return (onward("z", k, Z) if i == 0 else []) + onward("x", i, X)
    return (onward("x", i, X) if k == 0 else []) + onward("z", k, Z)


R_CORE = 0
R_SUM = numbered([name for name in sum_steps() if name[0] != "mul" and name not in (("a2", 0), ("b2", "mine"))], 4)
N_SUM = len(R_SUM)
R_G = 4 + N_SUM
R_STATE = R_G + 7
R_CROSS = R_STATE + 7
R_WAY = numbered([name + (way,) for name in gather_steps() for way in ways_on(name)], R_CROSS + 2 * Z)
N_ARRIVE = R_CROSS + 2 * Z + len(R_WAY)
S_CORE, S_SUM, S_G, S_STATE, S_WAY, S_CROSS = range(6)

L_ACTS = 0
L_COT = L_ACTS + 4
L_STATE = L_COT + 2
N_LOCAL = L_STATE + 4


def kernel(
    acts, cot, params, moment1, moment2, ema, live_rows, home, fresh, gathered,
    acts_buf, cot_buf, own, core_out, core_in, sum_out, sum_in,
    g_out, g_in, g_all, state, state_out, state_in, state_mine,
    position, order, send_sems, recv_sems, local_sems,
):
    dp = lax.axis_index("dp")
    y = lax.axis_index("section")
    c = lax.rem(dp, 2)
    z = lax.rem(lax.div(dp, 2), Z)
    x = lax.div(dp, 2 * Z)
    sign = 1 - 2 * c

    def xi(k):
        return lax.rem(x + sign * k + 2 * X, X)

    def zi(k):
        return lax.rem(z + sign * k + 2 * Z, Z)

    def at(xx, zz, cc, yy):
        return ((xx * Z + zz) * 2 + cc, yy)

    x_next, x_last = at(xi(1), z, c, y), at(xi(-1), z, c, y)
    z_next, z_last = at(x, zi(1), c, y), at(x, zi(-1), c, y)
    partner = at(x, z, 1 - c, y)
    others = []
    for dy in range(Y):
        for dc in range(2):
            if dy or dc:
                others.append((lax.rem(c + dc, 2), lax.rem(y + dy, Y)))

    barrier = pltpu.get_barrier_semaphore()
    greeted = [x_next, x_last, z_next, z_last] + [at(x, z, cc, yy) for cc, yy in others]
    for device in greeted:
        pl.semaphore_signal(barrier, inc=1, device_id=device, device_id_type=MESH)

    def local(src, dst, index):
        copy = pltpu.make_async_copy(src, dst, local_sems.at[index])
        copy.start()
        return copy

    def send(src, dst, device, group, number):
        copy = pltpu.make_async_remote_copy(
            src_ref=src, dst_ref=dst, send_sem=send_sems.at[group], recv_sem=recv_sems.at[number],
            device_id=device, device_id_type=MESH,
        )
        copy.start()
        return copy

    width = Z * PIECE
    cot_copies = []
    for half in range(2):
        column = pl.multiple_of(256 * lax.rem(c + half, 2), 256)
        cot_copies.append(
            local(cot.at[:, pl.ds(column, 256)], cot_buf.at[:, pl.ds(256 * half, 256)], L_COT + half)
        )

    def load_acts(t, offset):
        column = pl.multiple_of(width * lax.rem(x + offset, X), LANES)
        local(acts.at[:, pl.ds(column, width)], acts_buf.at[t], L_ACTS + t)

    load_acts(0, OFFSETS[0])
    state_copies = [
        local(ref, state.at[n], L_STATE + n) for n, ref in enumerate((params, moment1, moment2, ema))
    ]
    load_acts(1, OFFSETS[1])

    for copy in state_copies[:3]:
        copy.wait()

    @pl.loop(0, BLOCKS)
    def _(i):
        for n in range(3):
            for j in range(4):
                state_out[j // 2, n, j % 2, i] = state[n, pl.ds(i * 32 + j, 8, stride=4), :]

    pl.semaphore_wait(barrier, len(greeted))

    for copy in cot_copies:
        copy.wait()

    mine = 2 * y + c

    def spread(out, into, group, base):
        into[mine] = out[c]
        return [
            send(out.at[cc], into.at[mine], at(x, z, cc, yy), group, base + n)
            for n, (cc, yy) in enumerate(others)
        ]

    state_moves = spread(state_out, state_in, S_STATE, R_STATE)

    def core_copy(t):
        return pltpu.make_async_remote_copy(
            src_ref=core_out.at[t], dst_ref=core_in.at[t],
            send_sem=send_sems.at[S_CORE], recv_sem=recv_sems.at[R_CORE + t],
            device_id=partner, device_id_type=MESH,
        )

    def read_table():
        def section_row(s, carry):
            def block_entry(b, carry):
                counts, kept = carry[:Y], carry[Y:]
                keeper = home[s, b]
                rank = jnp.int32(0)
                for n in range(Y):
                    rank = jnp.where(keeper == n, counts[n], rank)
                place = keeper * BLOCKS + rank
                position[s * BLOCKS + b] = place
                counts = tuple(counts[n] + jnp.where(keeper == n, 1, 0) for n in range(Y))
                here = place - y * BLOCKS
                kept = tuple(jnp.where(here == n, s * BLOCKS + b, kept[n]) for n in range(BLOCKS))
                return counts + kept

            return lax.fori_loop(0, BLOCKS, block_entry, carry)

        table = lax.fori_loop(0, Y, section_row, (jnp.int32(0),) * (Y + BLOCKS))
        for n in range(BLOCKS):
            order[n] = table[Y + n]

    here = {"far": 0, "plus": 1 + c, "minus": 2 - c, "mine": 3}
    needed = {"far": (0,), "plus": (1, 2), "minus": (1, 2), "mine": (3,)}
    crossed, moving = {0}, {}

    def block(h, role, k):
        for t in needed[role]:
            if t not in crossed:
                core_copy(t).wait_recv()
                crossed.add(t)
        return own[here[role], h, zi(k)] + core_in[here[role], h, zi(k)].astype(F32)

    def taken(name):
        moving[name].wait_recv()
        return sum_in[R_SUM[name] - 4].astype(F32)

    def piece_copy(name, device):
        slot = R_SUM[name] - 4
        return pltpu.make_async_remote_copy(
            src_ref=sum_out.at[slot], dst_ref=sum_in.at[slot],
            send_sem=send_sems.at[S_SUM], recv_sem=recv_sems.at[R_SUM[name]],
            device_id=device, device_id_type=MESH,
        )

    def remember(name, device):
        moving[name] = piece_copy(name, device)

    def give(name, value, device):
        sum_out[R_SUM[name] - 4] = value.astype(BF16)
        piece_copy(name, device).start()
        remember(name, device)

    def along_x(role):
        return x_last if role == "minus" else x_next

    def along_z(k):
        return z_next if k > 0 else z_last

    early = [("b1", "far", 4), ("b1", "far", -3)] + [("a1", "far", k) for k in CHAIN + (0,)]

    @pl.loop(0, X)
    def _(t):
        pltpu.make_async_copy(
            acts.at[:, pl.ds(0, width)], acts_buf.at[t], local_sems.at[L_ACTS + t]
        ).wait()

        @pl.when(t < X - 2)
        def _():
            load_acts(t + 2, lax.select(t == 0, OFFSETS[2], OFFSETS[3]))

        product = lax.dot_general(
            acts_buf[t], cot_buf[...], (((0,), (0,)), ((), ())), preferred_element_type=F32
        )
        for h in range(2):
            own[t, h] = product[:, LANES * h : LANES * (h + 1)].reshape(Z, PIECE, LANES)
            other = product[:, 256 + LANES * h : 256 + LANES * (h + 1)]
            core_out[t, h] = other.reshape(Z, PIECE, LANES).astype(BF16)
        core_copy(t).start()

        def send_early(names):
            for name in names:
                half, role, k = name
                value = block(0 if half == "a1" else 1, role, k)
                sum_out[R_SUM[name] - 4] = value.astype(BF16)
                piece_copy(name, x_next if half == "a1" else along_z(k)).start()

        @pl.when(t == 1)
        def _():
            core_copy(0).wait_recv()
            send_early(early[:6])

        @pl.when(t == 2)
        def _():
            send_early(early[6:])

    for name in early:
        remember(name, x_next if name[0] == "a1" else along_z(name[2]))

    def collect():
        for copy in state_moves:
            copy.wait_recv()

        @pl.loop(0, BLOCKS)
        def _(b):
            place = position[y * BLOCKS + b]
            keeper = lax.div(place, BLOCKS)
            rank = place - keeper * BLOCKS
            for cc in range(2):
                for n in range(3):
                    for jj in range(2):
                        state_mine[n, jj, cc, b] = state_in[2 * keeper + cc, n, jj, rank]

    for step, name in enumerate(in_order(sum_steps())[0]):
        if step == 40:
            read_table()
        if step == len(sum_steps()) - 3:
            collect()
        if name[0] == "mul" or name in early:
            continue
        if name[0] == "a1":
            _, role, k = name
            value = block(0, role, k)
            if role == "plus":
                value = value + taken(("a1", "far", k))
            give(name, value, along_x(role))
        elif name[0] == "a2":
            k = name[1]
            value = block(0, "mine", k) + taken(("a1", "minus", k)) + taken(("a1", "plus", k))
            for earlier in (1, -1) if k == 0 else () if before(k) is None else (before(k),):
                value = value + taken(("a2", earlier))
            if k == 0:
                sum_a = value
            else:
                give(name, value, along_z(k))
        elif name[0] == "b1":
            _, role, k = name
            value = block(1, role, k)
            if before(k) is not None:
                value = value + taken(("b1", role, before(k)))
            give(name, value, along_z(k))
        else:
            role = name[1]
            value = block(1, role, 0) + taken(("b1", role, 1)) + taken(("b1", role, -1))
            for earlier in {"plus": ("far",), "mine": ("plus", "minus")}.get(role, ()):
                value = value + taken(("b2", earlier))
            if role == "mine":
                sum_b = value
            else:
                give(name, value, along_x(role))

    corr_one = 1.0 - 0.9**STEP
    corr_two = 1.0 - 0.99**STEP
    tile = lax.broadcasted_iota(jnp.int32, (8, LANES), 0)

    def adam(p, m1, m2, grads, alive):
        first = jnp.where(alive, 0.9 * m1 + 0.1 * grads, m1)
        second = jnp.where(alive, 0.99 * m2 + 0.01 * grads * grads, m2)
        stepped = p - 0.0025 * (first / corr_one) / (jnp.sqrt(second / corr_two) + 1e-08)
        return jnp.where(alive, stepped, p), first, second

    sums = [value.astype(BF16).astype(F32) for value in (sum_a, sum_b)]
    limit = live_rows[y] - (dp - c) * (4 * HALF)
    row = lax.broadcasted_iota(jnp.int32, (PIECE, LANES), 0) * 4
    for jj in range(2):
        p, m1, m2 = (state_mine[n, jj].reshape(PIECE, LANES) for n in range(3))
        updated, _, _ = adam(p, m1, m2, sums[jj], row + (2 * c + jj) < limit)
        gathered[2 * c + jj, x, z] = updated.astype(BF16)

    def send_gradient():
        for cc in range(2):
            rows = slice(HALF * cc, HALF * (cc + 1))
            g_out[cc] = jnp.concatenate([value[rows] for value in sums], axis=0).astype(BF16)
        return spread(g_out, g_in, S_G, R_G)

    def update_kept(gradient_moves):
        for copy in gradient_moves:
            copy.wait_recv()
        state_copies[3].wait()
        for s in range(Y):
            for cc in range(2):
                value = g_in[2 * s + cc].astype(F32)
                for jj in range(2):
                    rows = value[HALF * jj : HALF * (jj + 1)]
                    g_all[2 * cc + jj, BLOCKS * s : BLOCKS * (s + 1)] = rows.reshape(BLOCKS, 8, LANES)

        @pl.loop(0, BLOCKS)
        def _(i):
            f = order[i]
            s = lax.div(f, BLOCKS)
            b = f - s * BLOCKS
            limit = live_rows[s] - (dp * (4 * HALF) + b * 32)
            generator = tile * 0 + s < N_GEN
            for j in range(4):
                rows = pl.ds(i * 32 + j, 8, stride=4)
                alive = tile * 4 + j < limit
                p, m1, m2, average = (state[n, rows, :] for n in range(4))
                updated, first, second = adam(p, m1, m2, g_all[j, f], alive)
                averaged = jnp.where(generator, 0.995 * average + 0.005 * updated, average)
                for n, value in enumerate((updated, first, second, averaged)):
                    fresh[n, rows, :] = value

    ja, jb = 2 * c, 2 * c + 1
    halves = {"wa": ja, "wb": jb}
    ways = {"z_next": z_next, "z_last": z_last, "x_next": x_next, "x_last": x_last}

    def go(name, way):
        _, i, k = name
        ref = gathered.at[halves[name[0]], xi(i), zi(k)]
        moving[name + (way,)] = send(ref, ref, ways[way], S_WAY, R_WAY[name + (way,)])

    def comes(name, axis, i):
        back = i + 1 if i < 0 else i - 1
        at_sender = (name[0], back, name[2]) if axis == "x" else (name[0], name[1], back)
        moving[at_sender + (axis + ("_next" if i < 0 else "_last"),)].wait_recv()

    seen, crossing = [], {}

    def cross(half, k):
        ref = gathered.at[halves[half], :, zi(k)]
        crossing[half, k] = send(ref, ref, partner, S_CROSS, R_CROSS + len(crossing))

    def crossed_over(half, k):
        crossing[half, k].wait_recv()

    gather_order = in_order(gather_steps())[0]
    last_sent = max(step for step, name in enumerate(gather_order) if ways_on(name))
    for step, name in enumerate(gather_order):
        if step == 6:
            gradient_moves = send_gradient()
        if step == last_sent + 1:
            update_kept(gradient_moves)
        half, i, k = name
        first, second = (("z", k), ("x", i)) if half == "wa" else (("x", i), ("z", k))
        if second[1] != 0:
            comes(name, *second)
        elif first[1] != 0:
            comes(name, *first)
        for way in ways_on(name):
            go(name, way)
        seen.append(name)
        if sum(n[0] == half and n[2] == k for n in seen) == X:
            cross(half, k)

    for column in crossing:
        crossed_over(*column)

    for group, ref in (
        (S_CORE, core_out), (S_SUM, sum_out), (S_G, g_in.at[pl.ds(0, 7)]), (S_STATE, state_in.at[pl.ds(0, 7)]),
        (S_WAY, sum_out), (S_CROSS, gathered.at[pl.ds(0, 2)]),
    ):
        pltpu.make_async_copy(ref, ref, send_sems.at[group]).wait()


def write_out(fresh, gathered, new_params, new_moment1, new_moment2, new_ema, weights, sems):
    moves = [
        (gathered.at[j, xx], weights.at[xx, :, :, pl.ds(LANES * j, LANES)]) for xx in range(X) for j in range(4)
    ]
    moves += [(fresh.at[n], ref) for n, ref in enumerate((new_params, new_moment1, new_moment2, new_ema))]
    copies = [pltpu.make_async_copy(source, target, sems.at[n]) for n, (source, target) in enumerate(moves)]
    for copy in copies:
        copy.start()
    for copy in copies:
        copy.wait()


def body(acts, grad_out, params, moment1, moment2, ema, live_rows, home):
    tokens = acts.shape[1]
    rows = (4 * HALF, LANES)
    any_space = pl.BlockSpec(memory_space=pl.ANY)
    smem = pl.BlockSpec(memory_space=pltpu.SMEM)
    plane = (Z, PIECE, LANES)
    chunk = (PIECE, LANES)
    outs = pl.pallas_call(
        kernel,
        out_shape=[
            pltpu.VMEM((4,) + rows, F32),
            pltpu.VMEM((4, X) + plane, BF16),
        ],
        in_specs=[any_space] * 6 + [smem] * 2,
        out_specs=[pl.BlockSpec(memory_space=pltpu.VMEM)] * 2,
        scratch_shapes=[
            pltpu.VMEM((X, tokens, Z * PIECE), BF16),
            pltpu.VMEM((tokens, 4 * LANES), BF16),
            pltpu.VMEM((X, 2) + plane, F32),
            pltpu.VMEM((X, 2) + plane, BF16),
            pltpu.VMEM((X, 2) + plane, BF16),
            pltpu.VMEM((N_SUM,) + chunk, BF16),
            pltpu.VMEM((N_SUM,) + chunk, BF16),
            pltpu.VMEM((2,) + chunk, BF16),
            pltpu.VMEM((2 * Y,) + chunk, BF16),
            pltpu.VMEM((4, Y * BLOCKS, 8, LANES), F32),
            pltpu.VMEM((4,) + rows, F32),
            pltpu.VMEM((2, 3, 2, BLOCKS, 8, LANES), F32),
            pltpu.VMEM((2 * Y, 3, 2, BLOCKS, 8, LANES), F32),
            pltpu.VMEM((3, 2, 2, BLOCKS, 8, LANES), F32),
            pltpu.SMEM((Y * BLOCKS,), jnp.int32),
            pltpu.SMEM((BLOCKS,), jnp.int32),
            pltpu.SemaphoreType.DMA((S_CROSS + 1,)),
            pltpu.SemaphoreType.DMA((N_ARRIVE,)),
            pltpu.SemaphoreType.DMA((N_LOCAL,)),
        ],
        compiler_params=pltpu.CompilerParams(
            collective_id=0, has_side_effects=True, vmem_limit_bytes=57 * 2**20
        ),
    )(acts[0], grad_out[0], params[0], moment1[0], moment2[0], ema[0], live_rows, home)
    updated, first, second, averaged, weights = pl.pallas_call(
        write_out,
        out_shape=[jax.ShapeDtypeStruct(rows, F32)] * 4
        + [jax.ShapeDtypeStruct((X, Z, PIECE, 4 * LANES), BF16)],
        in_specs=[pl.BlockSpec(memory_space=pltpu.VMEM)] * 2,
        out_specs=[any_space] * 5,
        scratch_shapes=[
            pltpu.SemaphoreType.DMA((4 * X + 4,)),
        ],
        compiler_params=pltpu.CompilerParams(vmem_limit_bytes=40 * 2**20),
    )(*outs)
    return (
        updated[None], first[None], second[None], averaged[None],
        weights.reshape(1, X * Z * PIECE, 4 * LANES),
    )


def solution(mesh):
    split = P("section", "dp", None)
    in_specs = (split,) * 6 + (P(), P())
    out_specs = (split,) * 4 + (P("section", None, None),)
    return jax.shard_map(body, mesh=mesh, in_specs=in_specs, out_specs=out_specs, check_vma=False)
```
